128 devices in a mesh: tm: 8 (over x, core), space: 16 (over z, y).
Axes of the slice: x: 4, y: 4, z: 4, core: 2. Of those that a mesh axis runs over, the one named last changes fastest.
Arguments:
- thermal_reading: bfloat16 [32, 1440, 2048], P(None, 'space', 'tm'), may hold values from -140 to 140
- moisture_content: bfloat16 [32, 1440, 2048], P(None, 'space', 'tm'), may hold values from -160 to 160
- gram_eigenvector_columns: float32 [2048, 64], replicated, may hold values from -0.125 to 0.125
- marine_indicator: int32 [32, 1440], P('tm', 'space'), may hold values 0 or 1
Outputs:
- correlation: float32 [32, 1440, 64], P('tm', 'space')
The draws below stay inside these ranges and needn't reach their ends.
All inputs are finite; a program needn't handle non-finite values. No bound on the sum of `marine_indicator` on one device may be relied on, other than what follows from the above.
Results may differ from the reference program's by a relative error of at most 0.0007.
Values may be sent and summed in bfloat16 or wider, within the bound.
No kernel may reach another device: no remote copies, remote signals or barrier semaphores. Data moves between devices by JAX's collectives and lax.ppermute only.
A program may use at most 64 MiB of HBM per device.

```python
import math
import jax
import jax.numpy as jnp
from jax import lax

STEPS = 2048
MODES = 64
NLAT = 32
NLON = 1440


def field_pair(key):
    starting_value = jax.random.fold_in(key, 7301)
    lat_axis = (jnp.arange(NLAT, dtype=jnp.float32)[:, None, None] + 0.5) / NLAT
    lon_axis = jnp.arange(NLON, dtype=jnp.float32)[None, :, None] / NLON
    hours = jnp.arange(STEPS, dtype=jnp.float32)[None, None, :]
    signal = jnp.zeros((NLAT, NLON, STEPS), jnp.float32)
    for wave_index in range(8):
        subkeys = jax.random.split(jax.random.fold_in(starting_value, wave_index), 5)
        number = jax.random.randint(subkeys[0], (), 1, 8).astype(jnp.float32)
        period = jnp.exp(jax.random.uniform(subkeys[1], (), minval=math.log(12.0), maxval=math.log(1500.0)))
        phase_shift = jax.random.uniform(subkeys[2], (), minval=-math.pi, maxval=math.pi)
        center = jax.random.uniform(subkeys[3], ())
        height = jax.random.uniform(subkeys[4], (), minval=0.5, maxval=1.0)
        envelope = height * jnp.exp(-jnp.square((lat_axis - center) / 0.3))
        signal = signal + envelope * jnp.cos(2.0 * math.pi * (number * lon_axis - hours / period) + phase_shift)
    shape = (NLAT, NLON, STEPS)
    lattice_dimensions = (NLAT, NLON, 1)
    noise = jnp.clip(0.8 * jax.random.normal(jax.random.fold_in(starting_value, 101), shape), -3.2, 3.2)
    hum_noise = jnp.clip(0.6 * jax.random.normal(jax.random.fold_in(starting_value, 102), shape), -2.4, 2.4)
    coupling = jax.random.uniform(jax.random.fold_in(starting_value, 103), lattice_dimensions, minval=-1.0, maxval=1.0)
    thermal_spread_divisor = jnp.exp(jax.random.uniform(jax.random.fold_in(starting_value, 104), lattice_dimensions, minval=0.0, maxval=math.log(10.0)))
    hum_scale = jnp.exp(jax.random.uniform(jax.random.fold_in(starting_value, 105), lattice_dimensions, minval=0.0, maxval=math.log(10.0)))
    thermal_mean_shift = jax.random.uniform(jax.random.fold_in(starting_value, 106), lattice_dimensions, minval=-20.0, maxval=20.0)
    hum_offset = jax.random.uniform(jax.random.fold_in(starting_value, 107), lattice_dimensions, minval=-20.0, maxval=20.0)
    anomaly_array = signal + noise
    thermal_reading = thermal_mean_shift + thermal_spread_divisor * anomaly_array
    moisture_content = hum_offset + hum_scale * (coupling * anomaly_array + hum_noise)
    return (thermal_reading, moisture_content)


def draw_thermal_reading(key, part):
    return field_pair(key)[0].astype(jnp.bfloat16)


def draw_moisture_content(key, part):
    return field_pair(key)[1].astype(jnp.bfloat16)


def touch_ends(entries, own_key, smallest, high):
    place = [jax.random.randint(jax.random.fold_in(own_key, axis), (), 0, length) for axis, length in enumerate(entries.shape)]
    widest = entries.shape.index(max(entries.shape))
    beside = place[:widest] + [(place[widest] + 1) % entries.shape[widest]] + place[widest + 1:]
    return entries.at[tuple(place)].set(smallest).at[tuple(beside)].set(high)


def normal_values(own_key, dims, deviation, bound, held_as=jnp.bfloat16):
    entries = jax.random.normal(own_key, dims, jnp.float32) * deviation
    return jnp.minimum(jnp.maximum(entries, -bound), bound).astype(held_as)


def setup_inputs(seed: int = 0) -> dict:
    seeds = jax.random.split(jax.random.key(seed), 5)
    thermal_reading = draw_thermal_reading(jax.random.fold_in(seeds[4], 71), 0)
    moisture_content = draw_moisture_content(jax.random.fold_in(seeds[4], 71), 0)
    gram_eigenvector_columns = normal_values(seeds[2], (STEPS, MODES), STEPS ** -0.5, 0.125, jnp.float32)
    marine_indicator = touch_ends((jax.random.randint(seeds[3], (NLAT, NLON), 0, 3) < 2).astype(jnp.int32), jax.random.fold_in(seeds[3], 1), 0, 1)
    return dict(thermal_reading=thermal_reading, moisture_content=moisture_content, gram_eigenvector_columns=gram_eigenvector_columns, marine_indicator=marine_indicator)


def zscore(values):
    values = values.astype(jnp.float32)
    average = lax.optimization_barrier(jnp.mean(values, axis=-1, keepdims=True))
    centered = values - average
    return centered * lax.rsqrt(lax.optimization_barrier(jnp.mean(centered * centered, axis=-1, keepdims=True)) + 1e-05)

def reference(thermal_reading, moisture_content, gram_eigenvector_columns, marine_indicator):
    rows = jnp.arange(NLAT, dtype=jnp.float32)
    latitude = ((rows + 0.5) / NLAT * 120.0 - 60.0) * (math.pi / 180.0)
    radical_value = jnp.sqrt(jnp.cos(latitude))

    def lone_record(inputs):
        temp_row, humid_row, mask_row, weight = inputs
        scaling = weight * mask_row.astype(jnp.float32)
        ztemp = (zscore(temp_row) * scaling[:, None]).astype(jnp.bfloat16)
        zhum = zscore(humid_row).astype(jnp.bfloat16)
        loadings = jnp.dot(ztemp, gram_eigenvector_columns, precision=lax.Precision.HIGHEST, preferred_element_type=jnp.float32)
        partial_value = jnp.dot(ztemp.astype(jnp.float32).T, loadings, precision=lax.Precision.HIGHEST)
        return (partial_value, zhum)
    running_accumulations, normalized_moisture_complete = lax.map(lone_record, (thermal_reading, moisture_content, marine_indicator, radical_value))
    pcs = lax.optimization_barrier(jnp.sum(running_accumulations, axis=0))
    pc_mean = lax.optimization_barrier(jnp.mean(pcs, axis=0, keepdims=True))
    pc_centered = pcs - pc_mean
    pcz = (pc_centered * lax.rsqrt(lax.optimization_barrier(jnp.mean(pc_centered * pc_centered, axis=0, keepdims=True)) + 1e-05)).astype(jnp.bfloat16)
    flat_hum = normalized_moisture_complete.reshape(NLAT * NLON, STEPS)
    summed = jnp.dot(flat_hum, pcz, preferred_element_type=jnp.float32).reshape(NLAT, NLON, MODES)
    factor = marine_indicator.astype(jnp.float32) / STEPS
    return summed * factor[:, :, None]
```

```python
import math

import jax
import jax.numpy as jnp
from jax import lax
from jax.sharding import PartitionSpec as P


def zscore(values):
    values = values.astype(jnp.float32)
    average = jnp.mean(values, axis=-1, keepdims=True)
    centered = values - average
    return centered * lax.rsqrt(jnp.mean(centered * centered, axis=-1, keepdims=True) + 1e-05)


def area_root(first_row, row_count, total_lat):
    rows = (first_row + jnp.arange(row_count, dtype=jnp.int32)).astype(jnp.float32)
    latitude = ((rows + 0.5) / total_lat * 120.0 - 60.0) * (math.pi / 180.0)
    return jnp.sqrt(jnp.cos(latitude))


BOTH = ("tm", "space")


def sum_over_devices(partial_t):
    modes, hours = partial_t.shape
    blocks = partial_t.reshape(modes // 8, 8, hours // 128, 128)
    blocks = blocks.transpose(0, 2, 1, 3).reshape(-1, 8, 128)
    got = lax.all_to_all(blocks, BOTH, 0, 0)
    mine = jnp.sum(got, axis=0, keepdims=True)
    every = lax.all_to_all(jnp.broadcast_to(mine, blocks.shape), BOTH, 0, 0)
    every = every.reshape(modes // 8, hours // 128, 8, 128).transpose(0, 2, 1, 3)
    return every.reshape(modes, hours)


def per_device(thermal_reading, moisture_content, gram_eigenvector_columns, marine_indicator):
    mask_float = marine_indicator.astype(jnp.float32)
    temp = lax.all_to_all(thermal_reading, "tm", split_axis=0, concat_axis=2, tiled=True)
    hum = lax.all_to_all(moisture_content, "tm", split_axis=0, concat_axis=2, tiled=True)
    zt_float = zscore(temp)
    zhum = zscore(hum).astype(jnp.bfloat16)
    lat_count, lon_count, hour_count = zt_float.shape
    total_lat = lat_count * lax.axis_size("tm")
    root = area_root(lax.axis_index("tm") * lat_count, lat_count, total_lat)
    scaling = root[:, None] * mask_float
    ztemp = (zt_float * scaling[:, :, None]).astype(jnp.bfloat16)
    flat_temp = ztemp.reshape(lat_count * lon_count, hour_count)
    loadings = jnp.dot(
        flat_temp,
        gram_eigenvector_columns,
        precision=lax.Precision.HIGHEST,
        preferred_element_type=jnp.float32,
    )
    partial_t = lax.dot_general(
        loadings,
        flat_temp,
        (((0,), (0,)), ((), ())),
        precision=lax.Precision.HIGHEST,
        preferred_element_type=jnp.float32,
    )
    pcs = sum_over_devices(partial_t)
    pc_centered = pcs - jnp.mean(pcs, axis=1, keepdims=True)
    pc_var = jnp.mean(pc_centered * pc_centered, axis=1, keepdims=True)
    pcz = (pc_centered * lax.rsqrt(pc_var + 1e-05)).astype(jnp.bfloat16)
    flat_hum = zhum.reshape(lat_count * lon_count, hour_count)
    summed = lax.dot_general(
        flat_hum, pcz, (((1,), (1,)), ((), ())), preferred_element_type=jnp.float32
    ).reshape(lat_count, lon_count, pcz.shape[0])
    factor = mask_float / hour_count
    return summed * factor[:, :, None]


def solution(mesh):
    in_specs = (P(None, "space", "tm"), P(None, "space", "tm"), P(), P("tm", "space"))
    out_specs = P("tm", "space", None)
    return jax.shard_map(
        per_device, mesh=mesh, in_specs=in_specs, out_specs=out_specs, check_vma=False
    )
```

```python
import math

import jax
import jax.numpy as jnp
from jax import lax
from jax.experimental import pallas as pl
from jax.experimental.pallas import tpu as pltpu
from jax.sharding import PartitionSpec as P

BOTH = ("tm", "space")
F32 = jnp.float32
BF16 = jnp.bfloat16
EPS = 1e-05
NT = (((1,), (1,)), ((), ()))
NN = (((1,), (0,)), ((), ()))


def params():
    return pltpu.CompilerParams(vmem_limit_bytes=40 * 1024 * 1024)


def row_chunks(rows, step):
    return [(start, min(step, rows - start)) for start in range(0, rows, step)]


def three_terms(x):
    high = x.astype(BF16)
    rest = x - high.astype(F32)
    middle = rest.astype(BF16)
    low = (rest - middle.astype(F32)).astype(BF16)
    return high, middle, low


def split_kernel(modes, e_ref, out_ref):
    for n, term in enumerate(three_terms(e_ref[...])):
        out_ref[n * modes : (n + 1) * modes, :] = term


def split_columns(columns_t):
    modes, hours = columns_t.shape
    return pl.pallas_call(
        lambda e_ref, out_ref: split_kernel(modes, e_ref, out_ref),
        out_shape=jax.ShapeDtypeStruct((3 * modes, hours), BF16),
        compiler_params=params(),
        cost_estimate=pl.CostEstimate(flops=0, bytes_accessed=5 * modes * hours * 2, transcendentals=0),
    )(columns_t)


def temp_kernel(t_ref, e_ref, w_ref, out_ref, z_ref):
    blocks, cells, width = t_ref.shape
    modes = out_ref.shape[0]
    hours = blocks * width
    for start, size in row_chunks(cells, 48):
        rows = slice(start, start + size)
        total = jnp.zeros((size, width), F32)
        for b in range(blocks):
            total = total + t_ref[b, rows, :].astype(F32)
        average = jnp.sum(total, axis=1, keepdims=True) / hours
        square = jnp.zeros((size, width), F32)
        for b in range(blocks):
            centered = t_ref[b, rows, :].astype(F32) - average
            square = square + centered * centered
        scale = lax.rsqrt(jnp.sum(square, axis=1, keepdims=True) / hours + EPS)
        weight = w_ref[rows, :]
        for b in range(blocks):
            centered = t_ref[b, rows, :].astype(F32) - average
            z_ref[b, rows, :] = ((centered * scale) * weight).astype(BF16)
    loadings = jnp.zeros((cells, 3 * modes), F32)
    for b in range(blocks):
        loadings = loadings + lax.dot_general(
            z_ref[b], e_ref[:, b * width : (b + 1) * width], NT, preferred_element_type=F32
        )
    turned = loadings.T
    turned = turned[:modes] + (turned[modes : 2 * modes] + turned[2 * modes :])
    stacked = jnp.concatenate(three_terms(turned), axis=0)
    for b in range(blocks):
        sums = lax.dot_general(stacked, z_ref[b], NN, preferred_element_type=F32)
        out_ref[:, b * width : (b + 1) * width] = sums[:modes] + (
            sums[modes : 2 * modes] + sums[2 * modes :]
        )


def temp_sums(temp, split, weight):
    blocks, cells, width = temp.shape
    modes = split.shape[0] // 3
    return pl.pallas_call(
        temp_kernel,
        out_shape=jax.ShapeDtypeStruct((modes, blocks * width), F32),
        scratch_shapes=[pltpu.VMEM((blocks, cells, width), BF16)],
        compiler_params=params(),
        cost_estimate=pl.CostEstimate(
            flops=12 * cells * modes * blocks * width,
            bytes_accessed=2 * temp.size + 2 * split.size,
            transcendentals=cells,
        ),
    )(temp, split, weight)


def hum_kernel(place_ref, *refs):
    pieces, out_ref = refs[:-1], refs[-1]
    _, lats, lons, width = pieces[0].shape
    count = 2 * len(pieces)
    for i in range(lats):
        total = jnp.zeros((lons, width), F32)
        for piece in pieces:
            for n in range(2):
                total = total + piece[n, i].astype(F32)
        average = jnp.sum(total, axis=1, keepdims=True) / (count * width)
        square = jnp.zeros((lons, width), F32)
        for piece in pieces:
            for n in range(2):
                centered = piece[n, i].astype(F32) - average
                square = square + centered * centered
        scale = lax.rsqrt(jnp.sum(square, axis=1, keepdims=True) / (count * width) + EPS)
        for p, piece in enumerate(pieces):
            for n in range(2):
                centered = piece[n, i].astype(F32) - average
                out_ref[place_ref[2 * p + n], i, :lons, :] = (centered * scale).astype(BF16)


def hum_scores(places, pieces):
    _, lats, lons, width = pieces[0].shape
    padded = -(-lons // 16) * 16
    return pl.pallas_call(
        hum_kernel,
        in_specs=[pl.BlockSpec(memory_space=pltpu.SMEM)]
        + [pl.BlockSpec(memory_space=pltpu.VMEM)] * len(pieces),
        out_shape=jax.ShapeDtypeStruct((2 * len(pieces), lats, padded, width), BF16),
        compiler_params=params(),
        cost_estimate=pl.CostEstimate(
            flops=0, bytes_accessed=16 * pieces[0].size * len(pieces), transcendentals=0
        ),
    )(places, *pieces)


def final_kernel(pcs_ref, z_ref, factor_ref, out_ref):
    octets, runs, _, _ = pcs_ref.shape
    blocks, lats, padded, width = z_ref.shape
    lons = out_ref.shape[2]
    hours = runs * 128
    rows = []
    for r in range(octets):
        pcs = jnp.concatenate([pcs_ref[r, c] for c in range(runs)], axis=1)
        centered = pcs - jnp.sum(pcs, axis=1, keepdims=True) / hours
        variance = jnp.sum(centered * centered, axis=1, keepdims=True) / hours
        rows.append(centered * lax.rsqrt(variance + EPS))
    pcz = jnp.concatenate(rows, axis=0).astype(BF16)
    for i in range(lats):
        total = jnp.zeros((padded, 8 * octets), F32)
        for b in range(blocks):
            total = total + lax.dot_general(
                z_ref[b, i], pcz[:, b * width : (b + 1) * width], NT, preferred_element_type=F32
            )
        out_ref[i] = total.T[:, :lons] * factor_ref[i : i + 1, :]


def correlate(pcs, scores, factor):
    lats, lons = factor.shape
    modes = pcs.shape[0] * pcs.shape[2]
    return pl.pallas_call(
        final_kernel,
        out_shape=jax.ShapeDtypeStruct((lats, modes, lons), F32),
        compiler_params=params(),
        cost_estimate=pl.CostEstimate(
            flops=2 * scores.size * modes, bytes_accessed=4 * pcs.size + 2 * scores.size, transcendentals=0
        ),
    )(pcs, scores, factor)


def area_root(rows, total_lat):
    latitude = ((rows.astype(F32) + 0.5) / total_lat * 120.0 - 60.0) * (math.pi / 180.0)
    return jnp.sqrt(jnp.cos(latitude))


def per_device(thermal_reading, moisture_content, gram_eigenvector_columns, marine_indicator):
    total_lat, lons, width = thermal_reading.shape
    lats = marine_indicator.shape[0]
    hours, modes = gram_eigenvector_columns.shape
    members = lax.axis_size("tm")
    chips = members // 2
    me = lax.axis_index("tm")
    chip, core = lax.div(me, 2), lax.rem(me, 2)
    to_core = [(n, n ^ 1) for n in range(members)]
    to_chip = [[(n, (n + 2 * d) % members) for n in range(members)] for d in range(chips)]
    mask_float = marine_indicator.astype(F32)

    cells = total_lat * lons // members
    temp = thermal_reading.transpose(1, 0, 2).reshape(members, cells, width)
    temp = lax.all_to_all(temp, "tm", 0, 0)

    other = lax.ppermute(mask_float, "tm", to_core)
    pair = jnp.where(core == 0, jnp.stack([mask_float, other]), jnp.stack([other, mask_float]))
    whole = jnp.zeros((chips, 2, lats, lons), F32)
    for d in range(chips):
        got = pair if d == 0 else lax.ppermute(pair, "tm", to_chip[d])
        whole = lax.dynamic_update_slice(whole, got[None], (lax.rem(chip + chips - d, chips), 0, 0, 0))
    sea = lax.dynamic_slice(whole.reshape(total_lat, lons).T.reshape(-1), (me * cells,), (cells,))
    lat_of_cell = lax.rem(me * cells + jnp.arange(cells, dtype=jnp.int32), total_lat)
    weight = (area_root(lat_of_cell, total_lat) * sea)[:, None]

    hum = moisture_content.reshape(chips, 2, lats, lons, width)
    kept = lax.dynamic_index_in_dim(hum, core, 1, keepdims=False)
    sent = lax.dynamic_index_in_dim(hum, 1 - core, 1, keepdims=False)
    traded = lax.ppermute(sent, "tm", to_core)
    pieces = []
    for d in range(chips):
        target = lax.rem(chip + d, chips)
        pieces.append(
            jnp.stack(
                [
                    lax.dynamic_index_in_dim(kept, target, 0, keepdims=False),
                    lax.dynamic_index_in_dim(traded, target, 0, keepdims=False),
                ]
            )
        )

    split = split_columns(gram_eigenvector_columns.T)
    partial_t = temp_sums(temp, split, weight)

    partial_t, *pieces = lax.optimization_barrier((partial_t, *pieces))
    blocks = partial_t.reshape(modes // 8, 8, hours // 128, 128)
    blocks = blocks.transpose(0, 2, 1, 3).reshape(-1, 8, 128)
    got = lax.all_to_all(blocks, BOTH, 0, 0)
    pieces = [pieces[0]] + [lax.ppermute(pieces[d], "tm", to_chip[d]) for d in range(1, chips)]
    mine = jnp.sum(got, axis=0, keepdims=True)
    pcs = lax.all_to_all(jnp.broadcast_to(mine, blocks.shape), BOTH, 0, 0)
    pcs = pcs.reshape(modes // 8, hours // 128, 8, 128)

    places = []
    for d in range(chips):
        source = lax.rem(chip + chips - d, chips)
        places += [2 * source + core, 2 * source + 1 - core]
    scores = hum_scores(jnp.stack(places).astype(jnp.int32), pieces)
    return correlate(pcs, scores, mask_float / hours).transpose(0, 2, 1)


def solution(mesh):
    in_specs = (P(None, "space", "tm"), P(None, "space", "tm"), P(), P("tm", "space"))
    out_specs = P("tm", "space", None)
    return jax.shard_map(
        per_device, mesh=mesh, in_specs=in_specs, out_specs=out_specs, check_vma=False
    )
```

```python
import math

import jax
import jax.numpy as jnp
from jax import lax
from jax.experimental import pallas as pl
from jax.experimental.pallas import tpu as pltpu
from jax.sharding import PartitionSpec as P

BOTH = ("tm", "space")
F32 = jnp.float32
BF16 = jnp.bfloat16
EPS = 1e-05
NT = (((1,), (1,)), ((), ()))
NN = (((1,), (0,)), ((), ()))


def params():
    return pltpu.CompilerParams(vmem_limit_bytes=40 * 1024 * 1024)


def row_chunks(rows, step):
    return [(start, min(step, rows - start)) for start in range(0, rows, step)]


def three_terms(x):
    high = x.astype(BF16)
    rest = x - high.astype(F32)
    middle = rest.astype(BF16)
    low = (rest - middle.astype(F32)).astype(BF16)
    return high, middle, low


def split_kernel(modes, e_ref, out_ref):
    for n, term in enumerate(three_terms(e_ref[...])):
        out_ref[n * modes : (n + 1) * modes, :] = term


def split_columns(columns_t):
    modes, hours = columns_t.shape
    return pl.pallas_call(
        lambda e_ref, out_ref: split_kernel(modes, e_ref, out_ref),
        out_shape=jax.ShapeDtypeStruct((3 * modes, hours), BF16),
        compiler_params=params(),
        cost_estimate=pl.CostEstimate(flops=0, bytes_accessed=5 * modes * hours * 2, transcendentals=0),
    )(columns_t)


def temp_kernel(t_ref, e_ref, w_ref, out_ref, z_ref):
    blocks, cells, width = t_ref.shape
    modes = out_ref.shape[0]
    hours = blocks * width
    for start, size in row_chunks(cells, 48):
        rows = slice(start, start + size)
        total = jnp.zeros((size, width), F32)
        for b in range(blocks):
            total = total + t_ref[b, rows, :].astype(F32)
        average = jnp.sum(total, axis=1, keepdims=True) / hours
        square = jnp.zeros((size, width), F32)
        for b in range(blocks):
            centered = t_ref[b, rows, :].astype(F32) - average
            square = square + centered * centered
        scale = lax.rsqrt(jnp.sum(square, axis=1, keepdims=True) / hours + EPS)
        weight = w_ref[rows, :]
        for b in range(blocks):
            centered = t_ref[b, rows, :].astype(F32) - average
            z_ref[b, rows, :] = ((centered * scale) * weight).astype(BF16)
    loadings = jnp.zeros((cells, 3 * modes), F32)
    for b in range(blocks):
        loadings = loadings + lax.dot_general(
            z_ref[b], e_ref[:, b * width : (b + 1) * width], NT, preferred_element_type=F32
        )
    turned = loadings.T
    turned = turned[:modes] + (turned[modes : 2 * modes] + turned[2 * modes :])
    stacked = jnp.concatenate(three_terms(turned), axis=0)
    for b in range(blocks):
        sums = lax.dot_general(stacked, z_ref[b], NN, preferred_element_type=F32)
        out_ref[:, b * width : (b + 1) * width] = sums[:modes] + (
            sums[modes : 2 * modes] + sums[2 * modes :]
        )


def temp_sums(temp, split, weight):
    blocks, cells, width = temp.shape
    modes = split.shape[0] // 3
    return pl.pallas_call(
        temp_kernel,
        out_shape=jax.ShapeDtypeStruct((modes, blocks * width), F32),
        scratch_shapes=[pltpu.VMEM((blocks, cells, width), BF16)],
        compiler_params=params(),
        cost_estimate=pl.CostEstimate(
            flops=12 * cells * modes * blocks * width,
            bytes_accessed=2 * temp.size + 2 * split.size,
            transcendentals=cells,
        ),
    )(temp, split, weight)


def band_kernel(place_ref, h_ref, out_ref):
    lons, lats, width = h_ref.shape
    low = lax.broadcasted_iota(jnp.int32, (1, 8, width), 1) < 4
    for start, size in row_chunks(lons, 16):
        for top in range(0, lats, 16):
            tiles = h_ref[start : start + size, top : top + 16, :].astype(F32)
            for q in range(2):
                pairs = tiles[:, 8 * q : 8 * q + 8, :].reshape(size // 2, 2, 8, width)
                even, odd = pairs[:, 0], pairs[:, 1]
                first = jnp.where(low, even, jnp.roll(odd, 4, axis=1))
                second = jnp.where(low, jnp.roll(even, 4, axis=1), odd)
                rows = slice(4 * start, 4 * (start + size))
                band = top // 4 + 2 * q
                out_ref[place_ref[band], rows, :] = first.reshape(4 * size, width).astype(BF16)
                out_ref[place_ref[band + 1], rows, :] = second.reshape(4 * size, width).astype(BF16)


def lay_out_bands(places, hum):
    lons, lats, width = hum.shape
    return pl.pallas_call(
        band_kernel,
        in_specs=[pl.BlockSpec(memory_space=pltpu.SMEM), pl.BlockSpec(memory_space=pltpu.VMEM)],
        out_shape=jax.ShapeDtypeStruct((lats // 4, 4 * lons, width), BF16),
        compiler_params=params(),
        cost_estimate=pl.CostEstimate(flops=0, bytes_accessed=4 * hum.size, transcendentals=0),
    )(places, hum)


def hum_kernel(place_ref, *refs):
    pieces, out_ref = refs[:-1], refs[-1]
    count = len(pieces)
    _, cells, width = pieces[0].shape
    hours = count * width
    for start, size in row_chunks(cells, 48):
        rows = slice(start, start + size)
        total = jnp.zeros((size, width), F32)
        for piece in pieces:
            total = total + piece[0, rows, :].astype(F32)
        average = jnp.sum(total, axis=1, keepdims=True) / hours
        square = jnp.zeros((size, width), F32)
        for piece in pieces:
            centered = piece[0, rows, :].astype(F32) - average
            square = square + centered * centered
        scale = lax.rsqrt(jnp.sum(square, axis=1, keepdims=True) / hours + EPS)
        for n, piece in enumerate(pieces):
            centered = piece[0, rows, :].astype(F32) - average
            out_ref[place_ref[n], rows, :] = (centered * scale).astype(BF16)


def hum_scores(places, pieces):
    count = len(pieces)
    _, cells, width = pieces[0].shape
    return pl.pallas_call(
        hum_kernel,
        in_specs=[pl.BlockSpec(memory_space=pltpu.SMEM)]
        + [pl.BlockSpec(memory_space=pltpu.VMEM)] * count,
        out_shape=jax.ShapeDtypeStruct((count, cells, width), BF16),
        compiler_params=params(),
        cost_estimate=pl.CostEstimate(
            flops=0, bytes_accessed=16 * cells * width * count, transcendentals=0
        ),
    )(places, *pieces)


def final_kernel(pcs_ref, z_ref, factor_ref, out_ref, rows_ref):
    octets, runs, _, _ = pcs_ref.shape
    blocks, cells, width = z_ref.shape
    lats, modes, lons = out_ref.shape
    hours = runs * 128
    rows = []
    for r in range(octets):
        pcs = jnp.concatenate([pcs_ref[r, c] for c in range(runs)], axis=1)
        centered = pcs - jnp.sum(pcs, axis=1, keepdims=True) / hours
        variance = jnp.sum(centered * centered, axis=1, keepdims=True) / hours
        rows.append(centered * lax.rsqrt(variance + EPS))
    pcz = jnp.concatenate(rows, axis=0).astype(BF16)
    total = jnp.zeros((cells, modes), F32)
    for b in range(blocks):
        total = total + lax.dot_general(
            z_ref[b], pcz[:, b * width : (b + 1) * width], NT, preferred_element_type=F32
        )
    rows_ref[:, :modes] = total
    for i in range(lats):
        picked = rows_ref[pl.ds(i, lons, stride=lats), :]
        out_ref[i] = picked.T[:modes] * factor_ref[i : i + 1, :]


def correlate(pcs, scores, factor):
    lats, lons = factor.shape
    modes = pcs.shape[0] * pcs.shape[2]
    return pl.pallas_call(
        final_kernel,
        out_shape=jax.ShapeDtypeStruct((lats, modes, lons), F32),
        scratch_shapes=[pltpu.VMEM((lats * lons, 128), F32)],
        compiler_params=params(),
        cost_estimate=pl.CostEstimate(
            flops=2 * scores.size * modes, bytes_accessed=4 * pcs.size + 2 * scores.size, transcendentals=0
        ),
    )(pcs, scores, factor)


def area_root(rows, total_lat):
    latitude = ((rows.astype(F32) + 0.5) / total_lat * 120.0 - 60.0) * (math.pi / 180.0)
    return jnp.sqrt(jnp.cos(latitude))


def per_device(thermal_reading, moisture_content, gram_eigenvector_columns, marine_indicator):
    total_lat, lons, width = thermal_reading.shape
    lats = marine_indicator.shape[0]
    hours, modes = gram_eigenvector_columns.shape
    members = lax.axis_size("tm")
    chips = members // 2
    me = lax.axis_index("tm")
    chip, core = lax.div(me, 2), lax.rem(me, 2)
    to_core = [(n, n ^ 1) for n in range(members)]
    to_chip = [[(n, (n + 2 * d) % members) for n in range(members)] for d in range(chips)]
    mask_float = marine_indicator.astype(F32)

    cells = total_lat * lons // members
    temp = thermal_reading.transpose(1, 0, 2).reshape(members, cells, width)
    temp = lax.all_to_all(temp, "tm", 0, 0)

    other = lax.ppermute(mask_float, "tm", to_core)
    pair = jnp.where(core == 0, jnp.stack([mask_float, other]), jnp.stack([other, mask_float]))
    whole = jnp.zeros((chips, 2, lats, lons), F32)
    for d in range(chips):
        got = pair if d == 0 else lax.ppermute(pair, "tm", to_chip[d])
        whole = lax.dynamic_update_slice(whole, got[None], (lax.rem(chip + chips - d, chips), 0, 0, 0))
    sea = lax.dynamic_slice(whole.reshape(total_lat, lons).T.reshape(-1), (me * cells,), (cells,))
    lat_of_cell = lax.rem(me * cells + jnp.arange(cells, dtype=jnp.int32), total_lat)
    weight = (area_root(lat_of_cell, total_lat) * sea)[:, None]

    band = jnp.arange(members, dtype=jnp.int32)
    far = lax.rem(lax.div(band, 2) + chips - chip, chips)
    slot = lax.rem(band + core, 2)
    order = jnp.where(far == 0, 6 + slot, jnp.where(far == 1, slot, jnp.where(far == 2, 2 + 3 * slot, 3 + slot)))
    laid = lay_out_bands(order, moisture_content.transpose(1, 0, 2))
    ahead, behind, own = laid[0:3], laid[3:6], laid[6:8]
    own_traded = lax.ppermute(own[1:2], "tm", to_core)

    split = split_columns(gram_eigenvector_columns.T)
    partial_t = temp_sums(temp, split, weight)

    partial_t, ahead, behind = lax.optimization_barrier((partial_t, ahead, behind))
    blocks = partial_t.reshape(modes // 8, 8, hours // 128, 128)
    blocks = blocks.transpose(0, 2, 1, 3).reshape(-1, 8, 128)
    got = lax.all_to_all(blocks, BOTH, 0, 0)
    from_back = lax.ppermute(ahead, "tm", to_chip[1])
    from_front = lax.ppermute(behind, "tm", to_chip[chips - 1])
    mine = jnp.sum(got, axis=0, keepdims=True)
    mine, from_back, from_front = lax.optimization_barrier((mine, from_back, from_front))
    pcs = lax.all_to_all(jnp.broadcast_to(mine, blocks.shape), BOTH, 0, 0)
    pcs = pcs.reshape(modes // 8, hours // 128, 8, 128)
    far_first = lax.ppermute(from_back[2:3], "tm", to_chip[1])
    far_second = lax.ppermute(from_front[2:3], "tm", to_chip[chips - 1])
    back_traded = lax.ppermute(from_back[1:2], "tm", to_core)
    front_traded = lax.ppermute(from_front[1:2], "tm", to_core)
    far_traded = lax.ppermute(far_second, "tm", to_core)

    pieces = [own, own_traded, from_back, back_traded, from_front, front_traded, far_first, far_traded]
    step = lax.div(band, 2)
    distance = jnp.where(step == 0, 0, jnp.where(step == 1, chips - 1, step - 1))
    places = 2 * lax.rem(chip + distance, chips) + lax.rem(band + core, 2)
    scores = hum_scores(places, pieces)
    return correlate(pcs, scores, mask_float / hours).transpose(0, 2, 1)


def solution(mesh):
    in_specs = (P(None, "space", "tm"), P(None, "space", "tm"), P(), P("tm", "space"))
    out_specs = P("tm", "space", None)
    return jax.shard_map(
        per_device, mesh=mesh, in_specs=in_specs, out_specs=out_specs, check_vma=False
    )
```

```python
import math

import jax
import jax.numpy as jnp
from jax import lax
from jax.experimental import pallas as pl
from jax.experimental.pallas import tpu as pltpu
from jax.sharding import PartitionSpec as P

BOTH = ("tm", "space")
F32 = jnp.float32
BF16 = jnp.bfloat16
EPS = 1e-05
NT = (((1,), (1,)), ((), ()))
NN = (((1,), (0,)), ((), ()))


def params():
    return pltpu.CompilerParams(vmem_limit_bytes=16 * 1024 * 1024)


def row_chunks(rows, step):
    return [(start, min(step, rows - start)) for start in range(0, rows, step)]


def three_terms(x):
    high = x.astype(BF16)
    rest = x - high.astype(F32)
    middle = rest.astype(BF16)
    low = (rest - middle.astype(F32)).astype(BF16)
    return high, middle, low


def temp_kernel(t_ref, columns_ref, w_ref, out_ref, z_ref, e_ref, arrived):
    blocks, cells, width = t_ref.shape
    modes = out_ref.shape[0]
    hours = blocks * width
    fetch = pltpu.make_async_copy(columns_ref, e_ref, arrived)
    fetch.start()
    weights = jnp.broadcast_to(w_ref[...], (128, cells)).T
    for start, size in row_chunks(cells, 48):
        rows = slice(start, start + size)
        total = jnp.zeros((size, width), F32)
        for b in range(blocks):
            total = total + t_ref[b, rows, :].astype(F32)
        average = jnp.sum(total, axis=1, keepdims=True) / hours
        square = jnp.zeros((size, width), F32)
        for b in range(blocks):
            centered = t_ref[b, rows, :].astype(F32) - average
            square = square + centered * centered
        scale = lax.rsqrt(jnp.sum(square, axis=1, keepdims=True) / hours + EPS)
        weight = weights[rows, :1]
        for b in range(blocks):
            centered = t_ref[b, rows, :].astype(F32) - average
            z_ref[b, rows, :] = ((centered * scale) * weight).astype(BF16)
    fetch.wait()
    loadings = jnp.zeros((cells, 3 * modes), F32)
    for b in range(blocks):
        columns = jnp.concatenate(three_terms(e_ref[:, b * width : (b + 1) * width]), axis=0)
        loadings = loadings + lax.dot_general(z_ref[b], columns, NT, preferred_element_type=F32)
    turned = loadings.T
    turned = turned[:modes] + (turned[modes : 2 * modes] + turned[2 * modes :])
    stacked = jnp.concatenate(three_terms(turned), axis=0)
    for b in range(blocks):
        sums = lax.dot_general(stacked, z_ref[b], NN, preferred_element_type=F32)
        out_ref[:, b * width : (b + 1) * width] = sums[:modes] + (
            sums[modes : 2 * modes] + sums[2 * modes :]
        )


def temp_sums(temp, columns_t, weight):
    blocks, cells, width = temp.shape
    modes = columns_t.shape[0]
    return pl.pallas_call(
        temp_kernel,
        out_shape=jax.ShapeDtypeStruct((modes, blocks * width), F32),
        in_specs=[
            pl.BlockSpec(memory_space=pltpu.VMEM),
            pl.BlockSpec(memory_space=pl.ANY),
            pl.BlockSpec(memory_space=pltpu.VMEM),
        ],
        scratch_shapes=[
            pltpu.VMEM((blocks, cells, width), BF16),
            pltpu.VMEM(columns_t.shape, F32),
            pltpu.SemaphoreType.DMA,
        ],
        compiler_params=params(),
        cost_estimate=pl.CostEstimate(
            flops=12 * cells * modes * blocks * width,
            bytes_accessed=2 * temp.size + 4 * columns_t.size,
            transcendentals=cells,
        ),
    )(temp, columns_t, weight)


def sum_kernel(got_ref, out_ref):
    count = got_ref.shape[0]
    parts = []
    for n in range(8):
        part = got_ref[n]
        for m in range(n + 8, count, 8):
            part = part + got_ref[m]
        parts.append(part)
    while len(parts) > 1:
        parts = [parts[n] + parts[n + 1] for n in range(0, len(parts), 2)]
    for n in range(count):
        out_ref[n] = parts[0]


def sum_for_all(got):
    return pl.pallas_call(
        sum_kernel,
        out_shape=jax.ShapeDtypeStruct(got.shape, F32),
        compiler_params=params(),
        cost_estimate=pl.CostEstimate(flops=got.size, bytes_accessed=8 * got.size, transcendentals=0),
    )(got)


def band_kernel(place_ref, h_ref, out_ref):
    lons, lats, width = h_ref.shape
    low = lax.broadcasted_iota(jnp.int32, (1, 8, width), 1) < 4
    for start, size in row_chunks(lons, 16):
        for top in range(0, lats, 16):
            tiles = h_ref[start : start + size, top : top + 16, :].astype(F32)
            for q in range(2):
                pairs = tiles[:, 8 * q : 8 * q + 8, :].reshape(size // 2, 2, 8, width)
                even, odd = pairs[:, 0], pairs[:, 1]
                first = jnp.where(low, even, jnp.roll(odd, 4, axis=1))
                second = jnp.where(low, jnp.roll(even, 4, axis=1), odd)
                rows = slice(4 * start, 4 * (start + size))
                band = top // 4 + 2 * q
                out_ref[place_ref[band], rows, :] = first.reshape(4 * size, width).astype(BF16)
                out_ref[place_ref[band + 1], rows, :] = second.reshape(4 * size, width).astype(BF16)


def lay_out_bands(places, hum):
    lons, lats, width = hum.shape
    return pl.pallas_call(
        band_kernel,
        in_specs=[pl.BlockSpec(memory_space=pltpu.SMEM), pl.BlockSpec(memory_space=pltpu.VMEM)],
        out_shape=jax.ShapeDtypeStruct((lats // 4, 4 * lons, width), BF16),
        compiler_params=params(),
        cost_estimate=pl.CostEstimate(flops=0, bytes_accessed=4 * hum.size, transcendentals=0),
    )(places, hum)


def hum_kernel(place_ref, *refs):
    pieces, out_ref = refs[:-1], refs[-1]
    count = len(pieces)
    _, cells, width = pieces[0].shape
    hours = count * width
    for start, size in row_chunks(cells, 48):
        rows = slice(start, start + size)
        total = jnp.zeros((size, width), F32)
        for piece in pieces:
            total = total + piece[0, rows, :].astype(F32)
        average = jnp.sum(total, axis=1, keepdims=True) / hours
        square = jnp.zeros((size, width), F32)
        for piece in pieces:
            centered = piece[0, rows, :].astype(F32) - average
            square = square + centered * centered
        scale = lax.rsqrt(jnp.sum(square, axis=1, keepdims=True) / hours + EPS)
        for n, piece in enumerate(pieces):
            centered = piece[0, rows, :].astype(F32) - average
            out_ref[place_ref[n], rows, :] = (centered * scale).astype(BF16)


def hum_scores(places, pieces):
    count = len(pieces)
    _, cells, width = pieces[0].shape
    return pl.pallas_call(
        hum_kernel,
        in_specs=[pl.BlockSpec(memory_space=pltpu.SMEM)]
        + [pl.BlockSpec(memory_space=pltpu.VMEM)] * count,
        out_shape=jax.ShapeDtypeStruct((count, cells, width), BF16),
        compiler_params=params(),
        cost_estimate=pl.CostEstimate(
            flops=0, bytes_accessed=16 * cells * width * count, transcendentals=0
        ),
    )(places, *pieces)


def final_kernel(pcs_ref, z_ref, factor_ref, out_ref, rows_ref):
    octets, runs, _, _ = pcs_ref.shape
    blocks, cells, width = z_ref.shape
    lats, modes, lons = out_ref.shape
    hours = runs * 128
    rows = []
    for r in range(octets):
        pcs = jnp.concatenate([pcs_ref[r, c] for c in range(runs)], axis=1)
        centered = pcs - jnp.sum(pcs, axis=1, keepdims=True) / hours
        variance = jnp.sum(centered * centered, axis=1, keepdims=True) / hours
        rows.append(centered * lax.rsqrt(variance + EPS))
    pcz = jnp.concatenate(rows, axis=0).astype(BF16)
    total = jnp.zeros((cells, modes), F32)
    for b in range(blocks):
        total = total + lax.dot_general(
            z_ref[b], pcz[:, b * width : (b + 1) * width], NT, preferred_element_type=F32
        )
    rows_ref[:, :modes] = total
    for i in range(lats):
        picked = rows_ref[pl.ds(i, lons, stride=lats), :]
        out_ref[i] = picked.T[:modes] * factor_ref[i : i + 1, :]


def correlate(pcs, scores, factor):
    lats, lons = factor.shape
    modes = pcs.shape[0] * pcs.shape[2]
    return pl.pallas_call(
        final_kernel,
        out_shape=jax.ShapeDtypeStruct((lats, modes, lons), F32),
        scratch_shapes=[pltpu.VMEM((lats * lons, 128), F32)],
        compiler_params=params(),
        cost_estimate=pl.CostEstimate(
            flops=2 * scores.size * modes, bytes_accessed=4 * pcs.size + 2 * scores.size, transcendentals=0
        ),
    )(pcs, scores, factor)


def area_root(rows, total_lat):
    latitude = ((rows.astype(F32) + 0.5) / total_lat * 120.0 - 60.0) * (math.pi / 180.0)
    return jnp.sqrt(jnp.cos(latitude))


def per_device(thermal_reading, moisture_content, gram_eigenvector_columns, marine_indicator):
    total_lat, lons, width = thermal_reading.shape
    lats = marine_indicator.shape[0]
    hours, modes = gram_eigenvector_columns.shape
    members = lax.axis_size("tm")
    chips = members // 2
    me = lax.axis_index("tm")
    chip, core = lax.div(me, 2), lax.rem(me, 2)
    to_core = [(n, n ^ 1) for n in range(members)]
    to_chip = [[(n, (n + 2 * d) % members) for n in range(members)] for d in range(chips)]
    mask_float = marine_indicator.astype(F32)

    cells = total_lat * lons // members
    temp = thermal_reading.transpose(1, 0, 2).reshape(members, cells, width)
    temp = lax.all_to_all(temp, "tm", 0, 0)

    other = lax.ppermute(marine_indicator, "tm", to_core)
    pair = jnp.where(core == 0, jnp.stack([marine_indicator, other]), jnp.stack([other, marine_indicator]))
    whole = jnp.zeros((chips, 2, lats, lons), jnp.int32)
    for d in range(chips):
        got = pair if d == 0 else lax.ppermute(pair, "tm", to_chip[d])
        whole = lax.dynamic_update_slice(whole, got[None], (lax.rem(chip + chips - d, chips), 0, 0, 0))
    sea = lax.dynamic_slice(whole.reshape(total_lat, lons).T.reshape(-1), (me * cells,), (cells,))
    lat_of_cell = lax.rem(me * cells + jnp.arange(cells, dtype=jnp.int32), total_lat)
    weight = (area_root(lat_of_cell, total_lat) * sea.astype(F32))[None, :]

    band = jnp.arange(members, dtype=jnp.int32)
    far = lax.rem(lax.div(band, 2) + chips - chip, chips)
    slot = lax.rem(band + core, 2)
    order = jnp.where(far == 0, 6 + slot, jnp.where(far == 1, slot, jnp.where(far == 2, 2 + 3 * slot, 3 + slot)))
    laid = lay_out_bands(order, moisture_content.transpose(1, 0, 2))
    ahead, behind, own = laid[0:3], laid[3:6], laid[6:8]
    own_traded = lax.ppermute(own[1:2], "tm", to_core)

    weight, ahead, behind = lax.optimization_barrier((weight, ahead, behind))
    partial_t = temp_sums(temp, gram_eigenvector_columns.T, weight)
    blocks = partial_t.reshape(modes // 8, 8, hours // 128, 128)
    blocks = blocks.transpose(0, 2, 1, 3).reshape(-1, 8, 128)
    got = lax.all_to_all(blocks, BOTH, 0, 0)
    from_back = lax.ppermute(ahead, "tm", to_chip[1])
    from_front = lax.ppermute(behind, "tm", to_chip[chips - 1])
    far_first = lax.ppermute(from_back[2:3], "tm", to_chip[1])
    far_second = lax.ppermute(from_front[2:3], "tm", to_chip[chips - 1])
    back_traded = lax.ppermute(from_back[1:2], "tm", to_core)
    front_traded = lax.ppermute(from_front[1:2], "tm", to_core)
    got, far_first, far_second, back_traded, front_traded = lax.optimization_barrier(
        (got, far_first, far_second, back_traded, front_traded)
    )
    pcs = lax.all_to_all(sum_for_all(got), BOTH, 0, 0)
    pcs = pcs.reshape(modes // 8, hours // 128, 8, 128)
    far_traded = lax.ppermute(far_second, "tm", to_core)

    pieces = [own, own_traded, from_back, back_traded, from_front, front_traded, far_first, far_traded]
    step = lax.div(band, 2)
    distance = jnp.where(step == 0, 0, jnp.where(step == 1, chips - 1, step - 1))
    places = 2 * lax.rem(chip + distance, chips) + lax.rem(band + core, 2)
    scores = hum_scores(places, pieces)
    return correlate(pcs, scores, mask_float / hours).transpose(0, 2, 1)


def solution(mesh):
    in_specs = (P(None, "space", "tm"), P(None, "space", "tm"), P(), P("tm", "space"))
    out_specs = P("tm", "space", None)
    return jax.shard_map(
        per_device, mesh=mesh, in_specs=in_specs, out_specs=out_specs, check_vma=False
    )
```

```python
import math

import jax
import jax.numpy as jnp
from jax import lax
from jax.experimental import pallas as pl
from jax.experimental.pallas import tpu as pltpu
from jax.sharding import PartitionSpec as P

BOTH = ("tm", "space")
F32 = jnp.float32
BF16 = jnp.bfloat16
EPS = 1e-05
NT = (((1,), (1,)), ((), ()))
NN = (((1,), (0,)), ((), ()))


def params():
    return pltpu.CompilerParams(vmem_limit_bytes=16 * 1024 * 1024)


def row_chunks(rows, step):
    return [(start, min(step, rows - start)) for start in range(0, rows, step)]


def three_terms(x):
    high = x.astype(BF16)
    rest = x - high.astype(F32)
    middle = rest.astype(BF16)
    low = (rest - middle.astype(F32)).astype(BF16)
    return high, middle, low


def temp_kernel(t_ref, columns_ref, w_ref, out_ref, z_ref, e_ref, arrived):
    blocks, cells, width = t_ref.shape
    modes = out_ref.shape[0]
    hours = blocks * width
    fetch = pltpu.make_async_copy(columns_ref, e_ref, arrived)
    fetch.start()
    weights = jnp.broadcast_to(w_ref[...], (128, cells)).T
    for start, size in row_chunks(cells, 48):
        rows = slice(start, start + size)
        total = jnp.zeros((size, width), F32)
        for b in range(blocks):
            total = total + t_ref[b, rows, :].astype(F32)
        average = jnp.sum(total, axis=1, keepdims=True) / hours
        square = jnp.zeros((size, width), F32)
        for b in range(blocks):
            centered = t_ref[b, rows, :].astype(F32) - average
            square = square + centered * centered
        scale = lax.rsqrt(jnp.sum(square, axis=1, keepdims=True) / hours + EPS)
        weight = weights[rows, :1]
        for b in range(blocks):
            centered = t_ref[b, rows, :].astype(F32) - average
            z_ref[b, rows, :] = ((centered * scale) * weight).astype(BF16)
    fetch.wait()
    loadings = jnp.zeros((cells, 3 * modes), F32)
    for b in range(blocks):
        columns = jnp.concatenate(three_terms(e_ref[:, b * width : (b + 1) * width]), axis=0)
        loadings = loadings + lax.dot_general(z_ref[b], columns, NT, preferred_element_type=F32)
    turned = loadings.T
    turned = turned[:modes] + (turned[modes : 2 * modes] + turned[2 * modes :])
    stacked = jnp.concatenate(three_terms(turned), axis=0)
    for b in range(blocks):
        sums = lax.dot_general(stacked, z_ref[b], NN, preferred_element_type=F32)
        out_ref[:, b * width : (b + 1) * width] = sums[:modes] + (
            sums[modes : 2 * modes] + sums[2 * modes :]
        )


def temp_sums(temp, columns_t, weight):
    blocks, cells, width = temp.shape
    modes = columns_t.shape[0]
    return pl.pallas_call(
        temp_kernel,
        out_shape=jax.ShapeDtypeStruct((modes, blocks * width), F32),
        in_specs=[
            pl.BlockSpec(memory_space=pltpu.VMEM),
            pl.BlockSpec(memory_space=pltpu.HBM),
            pl.BlockSpec(memory_space=pltpu.VMEM),
        ],
        scratch_shapes=[
            pltpu.VMEM((blocks, cells, width), BF16),
            pltpu.VMEM(columns_t.shape, F32),
            pltpu.SemaphoreType.DMA,
        ],
        compiler_params=params(),
        cost_estimate=pl.CostEstimate(
            flops=12 * cells * modes * blocks * width,
            bytes_accessed=2 * temp.size + 4 * columns_t.size,
            transcendentals=cells,
        ),
    )(temp, columns_t, weight)


def sum_kernel(got_ref, out_ref):
    count = got_ref.shape[0]
    parts = []
    for n in range(8):
        part = got_ref[n]
        for m in range(n + 8, count, 8):
            part = part + got_ref[m]
        parts.append(part)
    while len(parts) > 1:
        parts = [parts[n] + parts[n + 1] for n in range(0, len(parts), 2)]
    for n in range(count):
        out_ref[n] = parts[0]


def sum_for_all(got):
    return pl.pallas_call(
        sum_kernel,
        out_shape=jax.ShapeDtypeStruct(got.shape, F32),
        compiler_params=params(),
        cost_estimate=pl.CostEstimate(flops=got.size, bytes_accessed=8 * got.size, transcendentals=0),
    )(got)


def band_kernel(place_ref, h_ref, out_ref):
    lons, lats, width = h_ref.shape
    low = lax.broadcasted_iota(jnp.int32, (1, 8, width), 1) < 4
    for start, size in row_chunks(lons, 16):
        for top in range(0, lats, 16):
            tiles = h_ref[start : start + size, top : top + 16, :].astype(F32)
            for q in range(2):
                pairs = tiles[:, 8 * q : 8 * q + 8, :].reshape(size // 2, 2, 8, width)
                even, odd = pairs[:, 0], pairs[:, 1]
                first = jnp.where(low, even, jnp.roll(odd, 4, axis=1))
                second = jnp.where(low, jnp.roll(even, 4, axis=1), odd)
                rows = slice(4 * start, 4 * (start + size))
                band = top // 4 + 2 * q
                out_ref[place_ref[band], rows, :] = first.reshape(4 * size, width).astype(BF16)
                out_ref[place_ref[band + 1], rows, :] = second.reshape(4 * size, width).astype(BF16)


def lay_out_bands(places, hum):
    lons, lats, width = hum.shape
    return pl.pallas_call(
        band_kernel,
        in_specs=[pl.BlockSpec(memory_space=pltpu.SMEM), pl.BlockSpec(memory_space=pltpu.VMEM)],
        out_shape=jax.ShapeDtypeStruct((lats // 4, 4 * lons, width), BF16),
        compiler_params=params(),
        cost_estimate=pl.CostEstimate(flops=0, bytes_accessed=4 * hum.size, transcendentals=0),
    )(places, hum)


def hum_kernel(place_ref, *refs):
    pieces, out_ref = refs[:-1], refs[-1]
    count = len(pieces)
    _, cells, width = pieces[0].shape
    hours = count * width
    for start, size in row_chunks(cells, 48):
        rows = slice(start, start + size)
        total = jnp.zeros((size, width), F32)
        for piece in pieces:
            total = total + piece[0, rows, :].astype(F32)
        average = jnp.sum(total, axis=1, keepdims=True) / hours
        square = jnp.zeros((size, width), F32)
        for piece in pieces:
            centered = piece[0, rows, :].astype(F32) - average
            square = square + centered * centered
        scale = lax.rsqrt(jnp.sum(square, axis=1, keepdims=True) / hours + EPS)
        for n, piece in enumerate(pieces):
            centered = piece[0, rows, :].astype(F32) - average
            out_ref[place_ref[n], rows, :] = (centered * scale).astype(BF16)


def hum_scores(places, pieces):
    count = len(pieces)
    _, cells, width = pieces[0].shape
    return pl.pallas_call(
        hum_kernel,
        in_specs=[pl.BlockSpec(memory_space=pltpu.SMEM)]
        + [pl.BlockSpec(memory_space=pltpu.VMEM)] * count,
        out_shape=jax.ShapeDtypeStruct((count, cells, width), BF16),
        compiler_params=params(),
        cost_estimate=pl.CostEstimate(
            flops=0, bytes_accessed=16 * cells * width * count, transcendentals=0
        ),
    )(places, *pieces)


def final_kernel(pcs_ref, z_ref, factor_ref, out_ref, rows_ref):
    octets, runs, _, _ = pcs_ref.shape
    blocks, cells, width = z_ref.shape
    lats, modes, lons = out_ref.shape
    hours = runs * 128
    rows = []
    for r in range(octets):
        pcs = jnp.concatenate([pcs_ref[r, c] for c in range(runs)], axis=1)
        centered = pcs - jnp.sum(pcs, axis=1, keepdims=True) / hours
        variance = jnp.sum(centered * centered, axis=1, keepdims=True) / hours
        rows.append(centered * lax.rsqrt(variance + EPS))
    pcz = jnp.concatenate(rows, axis=0).astype(BF16)
    total = jnp.zeros((cells, modes), F32)
    for b in range(blocks):
        total = total + lax.dot_general(
            z_ref[b], pcz[:, b * width : (b + 1) * width], NT, preferred_element_type=F32
        )
    rows_ref[:, :modes] = total
    for i in range(lats):
        picked = rows_ref[pl.ds(i, lons, stride=lats), :]
        out_ref[i] = picked.T[:modes] * factor_ref[i : i + 1, :]


def correlate(pcs, scores, factor):
    lats, lons = factor.shape
    modes = pcs.shape[0] * pcs.shape[2]
    return pl.pallas_call(
        final_kernel,
        out_shape=jax.ShapeDtypeStruct((lats, modes, lons), F32),
        scratch_shapes=[pltpu.VMEM((lats * lons, 128), F32)],
        compiler_params=params(),
        cost_estimate=pl.CostEstimate(
            flops=2 * scores.size * modes, bytes_accessed=4 * pcs.size + 2 * scores.size, transcendentals=0
        ),
    )(pcs, scores, factor)


def area_root(rows, total_lat):
    latitude = ((rows.astype(F32) + 0.5) / total_lat * 120.0 - 60.0) * (math.pi / 180.0)
    return jnp.sqrt(jnp.cos(latitude))


def per_device(thermal_reading, moisture_content, gram_eigenvector_columns, marine_indicator):
    total_lat, lons, width = thermal_reading.shape
    lats = marine_indicator.shape[0]
    hours, modes = gram_eigenvector_columns.shape
    members = lax.axis_size("tm")
    chips = members // 2
    me = lax.axis_index("tm")
    chip, core = lax.div(me, 2), lax.rem(me, 2)
    to_core = [(n, n ^ 1) for n in range(members)]
    to_chip = [[(n, (n + 2 * d) % members) for n in range(members)] for d in range(chips)]
    mask_float = marine_indicator.astype(F32)

    cells = total_lat * lons // members
    temp = thermal_reading.transpose(1, 0, 2).reshape(members, cells, width)
    temp = lax.all_to_all(temp, "tm", 0, 0)

    band = jnp.arange(members, dtype=jnp.int32)
    far = lax.rem(lax.div(band, 2) + chips - chip, chips)
    slot = lax.rem(band + core, 2)
    order = jnp.where(far == 0, 6 + slot, jnp.where(far == 1, slot, jnp.where(far == 2, 2 + 3 * slot, 3 + slot)))
    laid = lay_out_bands(order, moisture_content.transpose(1, 0, 2))
    ahead, behind, own = laid[0:3], laid[3:6], laid[6:8]
    own_traded = lax.ppermute(own[1:2], "tm", to_core)

    other = lax.ppermute(marine_indicator, "tm", to_core)
    pair = jnp.where(core == 0, jnp.stack([marine_indicator, other]), jnp.stack([other, marine_indicator]))
    pair, ahead, behind = lax.optimization_barrier((pair, ahead, behind))
    from_back = lax.ppermute(ahead, "tm", to_chip[1])
    from_front = lax.ppermute(behind, "tm", to_chip[chips - 1])
    whole = jnp.zeros((chips, 2, lats, lons), jnp.int32)
    for d in range(chips):
        got = pair if d == 0 else lax.ppermute(pair, "tm", to_chip[d])
        whole = lax.dynamic_update_slice(whole, got[None], (lax.rem(chip + chips - d, chips), 0, 0, 0))
    sea = lax.dynamic_slice(whole.reshape(total_lat, lons).T.reshape(-1), (me * cells,), (cells,))
    lat_of_cell = lax.rem(me * cells + jnp.arange(cells, dtype=jnp.int32), total_lat)
    weight = (area_root(lat_of_cell, total_lat) * sea.astype(F32))[None, :]

    partial_t = temp_sums(temp, gram_eigenvector_columns.T, weight)
    blocks = partial_t.reshape(modes // 8, 8, hours // 128, 128)
    blocks = blocks.transpose(0, 2, 1, 3).reshape(-1, 8, 128)
    got = lax.all_to_all(blocks, BOTH, 0, 0)
    far_first = lax.ppermute(from_back[2:3], "tm", to_chip[1])
    far_second = lax.ppermute(from_front[2:3], "tm", to_chip[chips - 1])
    back_traded = lax.ppermute(from_back[1:2], "tm", to_core)
    front_traded = lax.ppermute(from_front[1:2], "tm", to_core)
    got, far_first, far_second, back_traded, front_traded = lax.optimization_barrier(
        (got, far_first, far_second, back_traded, front_traded)
    )
    pcs = lax.all_to_all(sum_for_all(got), BOTH, 0, 0)
    pcs = pcs.reshape(modes // 8, hours // 128, 8, 128)
    far_traded = lax.ppermute(far_second, "tm", to_core)

    pieces = [own, own_traded, from_back, back_traded, from_front, front_traded, far_first, far_traded]
    step = lax.div(band, 2)
    distance = jnp.where(step == 0, 0, jnp.where(step == 1, chips - 1, step - 1))
    places = 2 * lax.rem(chip + distance, chips) + lax.rem(band + core, 2)
    scores = hum_scores(places, pieces)
    return correlate(pcs, scores, mask_float / hours).transpose(0, 2, 1)


def solution(mesh):
    in_specs = (P(None, "space", "tm"), P(None, "space", "tm"), P(), P("tm", "space"))
    out_specs = P("tm", "space", None)
    return jax.shard_map(
        per_device, mesh=mesh, in_specs=in_specs, out_specs=out_specs, check_vma=False
    )
```

```python
import math

import jax
import jax.numpy as jnp
from jax import lax
from jax.experimental import pallas as pl
from jax.experimental.pallas import tpu as pltpu
from jax.sharding import PartitionSpec as P

BOTH = ("tm", "space")
F32 = jnp.float32
BF16 = jnp.bfloat16
EPS = 1e-05
PACK_VMEM = 56 * 1024 * 1024
NT = (((1,), (1,)), ((), ()))
NN = (((1,), (0,)), ((), ()))


def params():
    return pltpu.CompilerParams(vmem_limit_bytes=16 * 1024 * 1024)


def row_chunks(rows, step):
    return [(start, min(step, rows - start)) for start in range(0, rows, step)]


def three_terms(x):
    high = x.astype(BF16)
    rest = x - high.astype(F32)
    middle = rest.astype(BF16)
    low = (rest - middle.astype(F32)).astype(BF16)
    return high, middle, low


def pack_kernel(in_ref, out_ref, done):
    halves, _, octets, _, _ = in_ref.shape
    copies = []
    for o in range(octets):
        for h in range(halves):
            copy = pltpu.make_async_copy(in_ref.at[h, :, o], out_ref.at[o, h], done.at[o * halves + h])
            copy.start()
            copies.append(copy)
    for copy in copies:
        copy.wait()


def pack_octets(field):
    halves, lons, octets, rows, width = field.shape
    return pl.pallas_call(
        pack_kernel,
        in_specs=[pl.BlockSpec(memory_space=pl.ANY)],
        out_specs=pl.BlockSpec(memory_space=pl.ANY),
        out_shape=jax.ShapeDtypeStruct((octets, halves, lons, rows, width), field.dtype),
        scratch_shapes=[pltpu.SemaphoreType.DMA((octets * halves,))],
        compiler_params=pltpu.CompilerParams(vmem_limit_bytes=PACK_VMEM),
        cost_estimate=pl.CostEstimate(flops=0, bytes_accessed=4 * field.size, transcendentals=0),
    )(field)


def temp_kernel(t_ref, columns_ref, w_ref, out_ref, z_ref, e_ref, sums_ref, arrived, stored):
    blocks, cells, width = t_ref.shape
    modes = out_ref.shape[0]
    hours = blocks * width
    fetch = pltpu.make_async_copy(columns_ref, e_ref, arrived)
    fetch.start()
    weights = jnp.broadcast_to(w_ref[...], (128, cells)).T
    for start, size in row_chunks(cells, 48):
        rows = slice(start, start + size)
        total = jnp.zeros((size, width), F32)
        for b in range(blocks):
            total = total + t_ref[b, rows, :].astype(F32)
        average = jnp.sum(total, axis=1, keepdims=True) / hours
        square = jnp.zeros((size, width), F32)
        for b in range(blocks):
            centered = t_ref[b, rows, :].astype(F32) - average
            square = square + centered * centered
        scale = lax.rsqrt(jnp.sum(square, axis=1, keepdims=True) / hours + EPS)
        weight = weights[rows, :1]
        for b in range(blocks):
            centered = t_ref[b, rows, :].astype(F32) - average
            z_ref[b, rows, :] = ((centered * scale) * weight).astype(BF16)
    fetch.wait()
    loadings = jnp.zeros((cells, 3 * modes), F32)
    for b in range(blocks):
        columns = jnp.concatenate(three_terms(e_ref[:, b * width : (b + 1) * width]), axis=0)
        loadings = loadings + lax.dot_general(z_ref[b], columns, NT, preferred_element_type=F32)
    turned = loadings.T
    turned = turned[:modes] + (turned[modes : 2 * modes] + turned[2 * modes :])
    stacked = jnp.concatenate(three_terms(turned), axis=0)
    copies = []
    for b in range(blocks):
        sums = lax.dot_general(stacked, z_ref[b], NN, preferred_element_type=F32)
        columns = slice(b * width, (b + 1) * width)
        sums_ref[:, columns] = sums[:modes] + (sums[modes : 2 * modes] + sums[2 * modes :])
        copy = pltpu.make_async_copy(sums_ref.at[:, columns], out_ref.at[:, columns], stored.at[b])
        copy.start()
        copies.append(copy)
    for copy in copies:
        copy.wait()


def temp_sums(temp, columns_t, weight):
    blocks, cells, width = temp.shape
    modes = columns_t.shape[0]
    return pl.pallas_call(
        temp_kernel,
        out_shape=jax.ShapeDtypeStruct((modes, blocks * width), F32),
        in_specs=[
            pl.BlockSpec(memory_space=pltpu.VMEM),
            pl.BlockSpec(memory_space=pltpu.HBM),
            pl.BlockSpec(memory_space=pltpu.VMEM),
        ],
        scratch_shapes=[
            pltpu.VMEM((blocks, cells, width), BF16),
            pltpu.VMEM(columns_t.shape, F32),
            pltpu.VMEM(columns_t.shape, F32),
            pltpu.SemaphoreType.DMA,
            pltpu.SemaphoreType.DMA((blocks,)),
        ],
        out_specs=pl.BlockSpec(memory_space=pl.ANY),
        compiler_params=params(),
        cost_estimate=pl.CostEstimate(
            flops=12 * cells * modes * blocks * width,
            bytes_accessed=2 * temp.size + 4 * columns_t.size,
            transcendentals=cells,
        ),
    )(temp, columns_t, weight)


def sum_kernel(got_ref, out_ref):
    count = got_ref.shape[0]
    parts = []
    for n in range(8):
        part = got_ref[n]
        for m in range(n + 8, count, 8):
            part = part + got_ref[m]
        parts.append(part)
    while len(parts) > 1:
        parts = [parts[n] + parts[n + 1] for n in range(0, len(parts), 2)]
    for n in range(count):
        out_ref[n] = parts[0]


def sum_for_all(got):
    return pl.pallas_call(
        sum_kernel,
        out_shape=jax.ShapeDtypeStruct(got.shape, F32),
        compiler_params=params(),
        cost_estimate=pl.CostEstimate(flops=got.size, bytes_accessed=8 * got.size, transcendentals=0),
    )(got)


def band_kernel(place_ref, h_ref, out_ref):
    lons, lats, width = h_ref.shape
    low = lax.broadcasted_iota(jnp.int32, (1, 8, width), 1) < 4
    for start, size in row_chunks(lons, 16):
        for top in range(0, lats, 16):
            tiles = h_ref[start : start + size, top : top + 16, :].astype(F32)
            for q in range(2):
                pairs = tiles[:, 8 * q : 8 * q + 8, :].reshape(size // 2, 2, 8, width)
                even, odd = pairs[:, 0], pairs[:, 1]
                first = jnp.where(low, even, jnp.roll(odd, 4, axis=1))
                second = jnp.where(low, jnp.roll(even, 4, axis=1), odd)
                rows = slice(4 * start, 4 * (start + size))
                band = top // 4 + 2 * q
                out_ref[place_ref[band], rows, :] = first.reshape(4 * size, width).astype(BF16)
                out_ref[place_ref[band + 1], rows, :] = second.reshape(4 * size, width).astype(BF16)


def lay_out_bands(places, hum):
    lons, lats, width = hum.shape
    return pl.pallas_call(
        band_kernel,
        in_specs=[pl.BlockSpec(memory_space=pltpu.SMEM), pl.BlockSpec(memory_space=pltpu.VMEM)],
        out_shape=jax.ShapeDtypeStruct((lats // 4, 4 * lons, width), BF16),
        compiler_params=params(),
        cost_estimate=pl.CostEstimate(flops=0, bytes_accessed=4 * hum.size, transcendentals=0),
    )(places, hum)


def hum_kernel(place_ref, *refs):
    pieces, out_ref = refs[:-1], refs[-1]
    count = len(pieces)
    _, cells, width = pieces[0].shape
    hours = count * width
    for start, size in row_chunks(cells, 48):
        rows = slice(start, start + size)
        total = jnp.zeros((size, width), F32)
        for piece in pieces:
            total = total + piece[0, rows, :].astype(F32)
        average = jnp.sum(total, axis=1, keepdims=True) / hours
        square = jnp.zeros((size, width), F32)
        for piece in pieces:
            centered = piece[0, rows, :].astype(F32) - average
            square = square + centered * centered
        scale = lax.rsqrt(jnp.sum(square, axis=1, keepdims=True) / hours + EPS)
        for n, piece in enumerate(pieces):
            centered = piece[0, rows, :].astype(F32) - average
            out_ref[place_ref[n], rows, :] = (centered * scale).astype(BF16)


def hum_scores(places, pieces):
    count = len(pieces)
    _, cells, width = pieces[0].shape
    return pl.pallas_call(
        hum_kernel,
        in_specs=[pl.BlockSpec(memory_space=pltpu.SMEM)]
        + [pl.BlockSpec(memory_space=pltpu.VMEM)] * count,
        out_shape=jax.ShapeDtypeStruct((count, cells, width), BF16),
        compiler_params=params(),
        cost_estimate=pl.CostEstimate(
            flops=0, bytes_accessed=16 * cells * width * count, transcendentals=0
        ),
    )(places, *pieces)


def final_kernel(pcs_ref, z_ref, factor_ref, out_ref, rows_ref):
    octets, runs, _, _ = pcs_ref.shape
    blocks, cells, width = z_ref.shape
    lats, modes, lons = out_ref.shape
    hours = runs * 128
    rows = []
    for r in range(octets):
        pcs = jnp.concatenate([pcs_ref[r, c] for c in range(runs)], axis=1)
        centered = pcs - jnp.sum(pcs, axis=1, keepdims=True) / hours
        variance = jnp.sum(centered * centered, axis=1, keepdims=True) / hours
        rows.append(centered * lax.rsqrt(variance + EPS))
    pcz = jnp.concatenate(rows, axis=0).astype(BF16)
    total = jnp.zeros((cells, modes), F32)
    for b in range(blocks):
        total = total + lax.dot_general(
            z_ref[b], pcz[:, b * width : (b + 1) * width], NT, preferred_element_type=F32
        )
    rows_ref[:, :modes] = total
    for i in range(lats):
        picked = rows_ref[pl.ds(i, lons, stride=lats), :]
        out_ref[i] = picked.T[:modes] * factor_ref[i : i + 1, :]


def correlate(pcs, scores, factor):
    lats, lons = factor.shape
    modes = pcs.shape[0] * pcs.shape[2]
    return pl.pallas_call(
        final_kernel,
        out_shape=jax.ShapeDtypeStruct((lats, modes, lons), F32),
        scratch_shapes=[pltpu.VMEM((lats * lons, 128), F32)],
        compiler_params=params(),
        cost_estimate=pl.CostEstimate(
            flops=2 * scores.size * modes, bytes_accessed=4 * pcs.size + 2 * scores.size, transcendentals=0
        ),
    )(pcs, scores, factor)


def area_root(rows, total_lat):
    latitude = ((rows.astype(F32) + 0.5) / total_lat * 120.0 - 60.0) * (math.pi / 180.0)
    return jnp.sqrt(jnp.cos(latitude))


def per_device(thermal_reading, moisture_content, gram_eigenvector_columns, marine_indicator):
    total_lat, lons, width = thermal_reading.shape
    lats = marine_indicator.shape[0]
    hours, modes = gram_eigenvector_columns.shape
    members = lax.axis_size("tm")
    chips = members // 2
    me = lax.axis_index("tm")
    chip, core = lax.div(me, 2), lax.rem(me, 2)
    to_core = [(n, n ^ 1) for n in range(members)]
    to_chip = [[(n, (n + 2 * d) % members) for n in range(members)] for d in range(chips)]
    mask_float = marine_indicator.astype(F32)

    half = lons // 2
    temp = thermal_reading.transpose(1, 0, 2).reshape(2, half, chips, 8, width)
    temp = pack_octets(temp).reshape(members, 8 * half, width)
    temp = lax.all_to_all(temp, "tm", 0, 0)

    band = jnp.arange(members, dtype=jnp.int32)
    far = lax.rem(lax.div(band, 2) + chips - chip, chips)
    slot = lax.rem(band + core, 2)
    order = jnp.where(far == 0, 6 + slot, jnp.where(far == 1, slot, jnp.where(far == 2, 2 + 3 * slot, 3 + slot)))
    laid = lay_out_bands(order, moisture_content.transpose(1, 0, 2))
    ahead, behind, own = laid[0:3], laid[3:6], laid[6:8]
    own_traded = lax.ppermute(own[1:2], "tm", to_core)

    other = lax.ppermute(marine_indicator, "tm", to_core)
    pair = jnp.where(core == 0, jnp.stack([marine_indicator, other]), jnp.stack([other, marine_indicator]))
    pair, ahead, behind = lax.optimization_barrier((pair, ahead, behind))
    from_back = lax.ppermute(ahead, "tm", to_chip[1])
    from_front = lax.ppermute(behind, "tm", to_chip[chips - 1])
    root = area_root(8 * chip + jnp.arange(8, dtype=jnp.int32), total_lat)
    scaling = root[:, None] * pair.reshape(8, lons).astype(F32)
    weight = lax.dynamic_slice(scaling.T, (core * half, 0), (half, 8)).reshape(1, 8 * half)
    weight, own_traded = lax.optimization_barrier((weight, own_traded))

    partial_t = temp_sums(temp, gram_eigenvector_columns.T, weight)
    blocks = partial_t.reshape(modes // 8, 8, hours // 128, 128)
    blocks = blocks.transpose(0, 2, 1, 3).reshape(-1, 8, 128)
    got = lax.all_to_all(blocks, BOTH, 0, 0)
    far_first = lax.ppermute(from_back[2:3], "tm", to_chip[1])
    far_second = lax.ppermute(from_front[2:3], "tm", to_chip[chips - 1])
    back_traded = lax.ppermute(from_back[1:2], "tm", to_core)
    front_traded = lax.ppermute(from_front[1:2], "tm", to_core)
    far_traded = lax.ppermute(far_second, "tm", to_core)
    got, far_first, far_traded, back_traded, front_traded = lax.optimization_barrier(
        (got, far_first, far_traded, back_traded, front_traded)
    )
    pcs = lax.all_to_all(sum_for_all(got), BOTH, 0, 0)
    pcs = pcs.reshape(modes // 8, hours // 128, 8, 128)

    pieces = [own, own_traded, from_back, back_traded, from_front, front_traded, far_first, far_traded]
    step = lax.div(band, 2)
    distance = jnp.where(step == 0, 0, jnp.where(step == 1, chips - 1, step - 1))
    places = 2 * lax.rem(chip + distance, chips) + lax.rem(band + core, 2)
    scores = hum_scores(places, pieces)
    return correlate(pcs, scores, mask_float / hours).transpose(0, 2, 1)


def solution(mesh):
    in_specs = (P(None, "space", "tm"), P(None, "space", "tm"), P(), P("tm", "space"))
    out_specs = P("tm", "space", None)
    return jax.shard_map(
        per_device, mesh=mesh, in_specs=in_specs, out_specs=out_specs, check_vma=False
    )
```

```python
import math

import jax
import jax.numpy as jnp
from jax import lax
from jax.experimental import pallas as pl
from jax.experimental.pallas import tpu as pltpu
from jax.sharding import PartitionSpec as P

BOTH = ("tm", "space")
F32 = jnp.float32
BF16 = jnp.bfloat16
EPS = 1e-05
PACK_VMEM = 56 * 1024 * 1024
NT = (((1,), (1,)), ((), ()))
NN = (((1,), (0,)), ((), ()))


def params():
    return pltpu.CompilerParams(vmem_limit_bytes=16 * 1024 * 1024)


def row_chunks(rows, step):
    return [(start, min(step, rows - start)) for start in range(0, rows, step)]


def three_terms(x):
    high = x.astype(BF16)
    rest = x - high.astype(F32)
    middle = rest.astype(BF16)
    low = (rest - middle.astype(F32)).astype(BF16)
    return high, middle, low


def pack_kernel(in_ref, out_ref, held, loaded, stored):
    halves, _, octets, _, _ = in_ref.shape
    places = [(o, h) for o in range(octets) for h in range(halves)]
    loads = [
        pltpu.make_async_copy(in_ref.at[h, :, o], held.at[o, h], loaded.at[n])
        for n, (o, h) in enumerate(places)
    ]
    stores = [
        pltpu.make_async_copy(held.at[o, h], out_ref.at[o, h], stored.at[n])
        for n, (o, h) in enumerate(places)
    ]
    for load in loads:
        load.start()
    for load, store in zip(loads, stores):
        load.wait()
        store.start()
    for store in stores:
        store.wait()


def pack_octets(field):
    halves, lons, octets, rows, width = field.shape
    shape = (octets, halves, lons, rows, width)
    return pl.pallas_call(
        pack_kernel,
        in_specs=[pl.BlockSpec(memory_space=pl.ANY)],
        out_specs=pl.BlockSpec(memory_space=pl.ANY),
        out_shape=jax.ShapeDtypeStruct(shape, field.dtype),
        scratch_shapes=[
            pltpu.VMEM(shape, field.dtype),
            pltpu.SemaphoreType.DMA((octets * halves,)),
            pltpu.SemaphoreType.DMA((octets * halves,)),
        ],
        compiler_params=pltpu.CompilerParams(vmem_limit_bytes=PACK_VMEM),
        cost_estimate=pl.CostEstimate(flops=0, bytes_accessed=4 * field.size, transcendentals=0),
    )(field)


def split_kernel(modes, e_ref, out_ref):
    for n, term in enumerate(three_terms(e_ref[...])):
        out_ref[n * modes : (n + 1) * modes, :] = term


def split_columns(columns_t):
    modes, hours = columns_t.shape
    return pl.pallas_call(
        lambda e_ref, out_ref: split_kernel(modes, e_ref, out_ref),
        out_shape=jax.ShapeDtypeStruct((3 * modes, hours), BF16),
        compiler_params=params(),
        cost_estimate=pl.CostEstimate(flops=0, bytes_accessed=5 * modes * hours * 2, transcendentals=0),
    )(columns_t)


def scores_kernel(t_ref, w_ref, z_ref):
    blocks, cells, width = t_ref.shape
    hours = blocks * width
    weights = jnp.broadcast_to(w_ref[...], (128, cells)).T
    for start, size in row_chunks(cells, 48):
        rows = slice(start, start + size)
        total = jnp.zeros((size, width), F32)
        for b in range(blocks):
            total = total + t_ref[b, rows, :].astype(F32)
        average = jnp.sum(total, axis=1, keepdims=True) / hours
        square = jnp.zeros((size, width), F32)
        for b in range(blocks):
            centered = t_ref[b, rows, :].astype(F32) - average
            square = square + centered * centered
        scale = lax.rsqrt(jnp.sum(square, axis=1, keepdims=True) / hours + EPS)
        weight = weights[rows, :1]
        for b in range(blocks):
            centered = t_ref[b, rows, :].astype(F32) - average
            z_ref[b, rows, :] = ((centered * scale) * weight).astype(BF16)


def sums_kernel(z_ref, e_ref, out_ref):
    blocks, cells, width = z_ref.shape
    modes = out_ref.shape[0]
    loadings = jnp.zeros((cells, 3 * modes), F32)
    for b in range(blocks):
        loadings = loadings + lax.dot_general(
            z_ref[b], e_ref[:, b * width : (b + 1) * width], NT, preferred_element_type=F32
        )
    turned = loadings.T
    turned = turned[:modes] + (turned[modes : 2 * modes] + turned[2 * modes :])
    stacked = jnp.concatenate(three_terms(turned), axis=0)
    for b in range(blocks):
        sums = lax.dot_general(stacked, z_ref[b], NN, preferred_element_type=F32)
        out_ref[:, b * width : (b + 1) * width] = sums[:modes] + (
            sums[modes : 2 * modes] + sums[2 * modes :]
        )


def temp_sums(temp, split, weight):
    blocks, cells, width = temp.shape
    modes = split.shape[0] // 3
    scores = pl.pallas_call(
        scores_kernel,
        out_shape=jax.ShapeDtypeStruct(temp.shape, BF16),
        compiler_params=params(),
        cost_estimate=pl.CostEstimate(
            flops=16 * temp.size, bytes_accessed=4 * temp.size, transcendentals=cells
        ),
    )(temp, weight)
    return pl.pallas_call(
        sums_kernel,
        out_shape=jax.ShapeDtypeStruct((modes, blocks * width), F32),
        compiler_params=params(),
        cost_estimate=pl.CostEstimate(
            flops=12 * cells * modes * blocks * width,
            bytes_accessed=2 * temp.size + 2 * split.size,
            transcendentals=0,
        ),
    )(scores, split)


def sum_kernel(got_ref, out_ref):
    count = got_ref.shape[0]
    parts = []
    for n in range(8):
        part = got_ref[n]
        for m in range(n + 8, count, 8):
            part = part + got_ref[m]
        parts.append(part)
    while len(parts) > 1:
        parts = [parts[n] + parts[n + 1] for n in range(0, len(parts), 2)]
    for n in range(count):
        out_ref[n] = parts[0]


def sum_for_all(got):
    return pl.pallas_call(
        sum_kernel,
        out_shape=jax.ShapeDtypeStruct(got.shape, F32),
        compiler_params=params(),
        cost_estimate=pl.CostEstimate(flops=got.size, bytes_accessed=8 * got.size, transcendentals=0),
    )(got)


def band_kernel(place_ref, h_ref, out_ref):
    lons, lats, width = h_ref.shape
    low = lax.broadcasted_iota(jnp.int32, (1, 8, width), 1) < 4
    for start, size in row_chunks(lons, 16):
        for top in range(0, lats, 16):
            tiles = h_ref[start : start + size, top : top + 16, :].astype(F32)
            for q in range(2):
                pairs = tiles[:, 8 * q : 8 * q + 8, :].reshape(size // 2, 2, 8, width)
                even, odd = pairs[:, 0], pairs[:, 1]
                first = jnp.where(low, even, jnp.roll(odd, 4, axis=1))
                second = jnp.where(low, jnp.roll(even, 4, axis=1), odd)
                rows = slice(4 * start, 4 * (start + size))
                band = top // 4 + 2 * q
                out_ref[place_ref[band], rows, :] = first.reshape(4 * size, width).astype(BF16)
                out_ref[place_ref[band + 1], rows, :] = second.reshape(4 * size, width).astype(BF16)


def lay_out_bands(places, hum):
    lons, lats, width = hum.shape
    return pl.pallas_call(
        band_kernel,
        in_specs=[pl.BlockSpec(memory_space=pltpu.SMEM), pl.BlockSpec(memory_space=pltpu.VMEM)],
        out_shape=jax.ShapeDtypeStruct((lats // 4, 4 * lons, width), BF16),
        compiler_params=params(),
        cost_estimate=pl.CostEstimate(flops=0, bytes_accessed=4 * hum.size, transcendentals=0),
    )(places, hum)


def hum_kernel(place_ref, *refs):
    pieces, out_ref = refs[:-1], refs[-1]
    count = len(pieces)
    _, cells, width = pieces[0].shape
    hours = count * width
    for start, size in row_chunks(cells, 48):
        rows = slice(start, start + size)
        total = jnp.zeros((size, width), F32)
        for piece in pieces:
            total = total + piece[0, rows, :].astype(F32)
        average = jnp.sum(total, axis=1, keepdims=True) / hours
        square = jnp.zeros((size, width), F32)
        for piece in pieces:
            centered = piece[0, rows, :].astype(F32) - average
            square = square + centered * centered
        scale = lax.rsqrt(jnp.sum(square, axis=1, keepdims=True) / hours + EPS)
        for n, piece in enumerate(pieces):
            centered = piece[0, rows, :].astype(F32) - average
            out_ref[place_ref[n], rows, :] = (centered * scale).astype(BF16)


def hum_scores(places, pieces):
    count = len(pieces)
    _, cells, width = pieces[0].shape
    return pl.pallas_call(
        hum_kernel,
        in_specs=[pl.BlockSpec(memory_space=pltpu.SMEM)]
        + [pl.BlockSpec(memory_space=pltpu.VMEM)] * count,
        out_shape=jax.ShapeDtypeStruct((count, cells, width), BF16),
        compiler_params=params(),
        cost_estimate=pl.CostEstimate(
            flops=0, bytes_accessed=16 * cells * width * count, transcendentals=0
        ),
    )(places, *pieces)


def final_kernel(pcs_ref, z_ref, factor_ref, out_ref, rows_ref):
    octets, runs, _, _ = pcs_ref.shape
    blocks, cells, width = z_ref.shape
    lats, modes, lons = out_ref.shape
    hours = runs * 128
    rows = []
    for r in range(octets):
        pcs = jnp.concatenate([pcs_ref[r, c] for c in range(runs)], axis=1)
        centered = pcs - jnp.sum(pcs, axis=1, keepdims=True) / hours
        variance = jnp.sum(centered * centered, axis=1, keepdims=True) / hours
        rows.append(centered * lax.rsqrt(variance + EPS))
    pcz = jnp.concatenate(rows, axis=0).astype(BF16)
    total = jnp.zeros((cells, modes), F32)
    for b in range(blocks):
        total = total + lax.dot_general(
            z_ref[b], pcz[:, b * width : (b + 1) * width], NT, preferred_element_type=F32
        )
    rows_ref[:, :modes] = total
    for i in range(lats):
        picked = rows_ref[pl.ds(i, lons, stride=lats), :]
        out_ref[i] = picked.T[:modes] * factor_ref[i : i + 1, :]


def correlate(pcs, scores, factor):
    lats, lons = factor.shape
    modes = pcs.shape[0] * pcs.shape[2]
    return pl.pallas_call(
        final_kernel,
        out_shape=jax.ShapeDtypeStruct((lats, modes, lons), F32),
        scratch_shapes=[pltpu.VMEM((lats * lons, 128), F32)],
        compiler_params=params(),
        cost_estimate=pl.CostEstimate(
            flops=2 * scores.size * modes, bytes_accessed=4 * pcs.size + 2 * scores.size, transcendentals=0
        ),
    )(pcs, scores, factor)


def area_root(rows, total_lat):
    latitude = ((rows.astype(F32) + 0.5) / total_lat * 120.0 - 60.0) * (math.pi / 180.0)
    return jnp.sqrt(jnp.cos(latitude))


def per_device(thermal_reading, moisture_content, gram_eigenvector_columns, marine_indicator):
    total_lat, lons, width = thermal_reading.shape
    lats = marine_indicator.shape[0]
    hours, modes = gram_eigenvector_columns.shape
    members = lax.axis_size("tm")
    chips = members // 2
    me = lax.axis_index("tm")
    chip, core = lax.div(me, 2), lax.rem(me, 2)
    to_core = [(n, n ^ 1) for n in range(members)]
    to_chip = [[(n, (n + 2 * d) % members) for n in range(members)] for d in range(chips)]
    mask_float = marine_indicator.astype(F32)

    half = lons // 2
    temp = thermal_reading.transpose(1, 0, 2).reshape(2, half, chips, 8, width)
    temp = pack_octets(temp).reshape(members, 8 * half, width)
    temp = lax.all_to_all(temp, "tm", 0, 0)

    band = jnp.arange(members, dtype=jnp.int32)
    far = lax.rem(lax.div(band, 2) + chips - chip, chips)
    slot = lax.rem(band + core, 2)
    order = jnp.where(far == 0, 6 + slot, jnp.where(far == 1, slot, jnp.where(far == 2, 2 + 3 * slot, 3 + slot)))
    laid = lay_out_bands(order, moisture_content.transpose(1, 0, 2))
    ahead, behind, own = laid[0:3], laid[3:6], laid[6:8]
    own_traded = lax.ppermute(own[1:2], "tm", to_core)

    other = lax.ppermute(marine_indicator, "tm", to_core)
    pair = jnp.where(core == 0, jnp.stack([marine_indicator, other]), jnp.stack([other, marine_indicator]))
    pair, ahead, behind = lax.optimization_barrier((pair, ahead, behind))
    from_back = lax.ppermute(ahead, "tm", to_chip[1])
    from_front = lax.ppermute(behind, "tm", to_chip[chips - 1])
    root = area_root(8 * chip + jnp.arange(8, dtype=jnp.int32), total_lat)
    scaling = root[:, None] * pair.reshape(8, lons).astype(F32)
    weight = lax.dynamic_slice(scaling.T, (core * half, 0), (half, 8)).reshape(1, 8 * half)

    partial_t = temp_sums(temp, split_columns(gram_eigenvector_columns.T), weight)
    blocks = partial_t.reshape(modes // 8, 8, hours // 128, 128)
    blocks = blocks.transpose(0, 2, 1, 3).reshape(-1, 8, 128)
    got = lax.all_to_all(blocks, BOTH, 0, 0)
    far_first = lax.ppermute(from_back[2:3], "tm", to_chip[1])
    far_second = lax.ppermute(from_front[2:3], "tm", to_chip[chips - 1])
    back_traded = lax.ppermute(from_back[1:2], "tm", to_core)
    front_traded = lax.ppermute(from_front[1:2], "tm", to_core)
    got, far_first, far_second, back_traded, front_traded = lax.optimization_barrier(
        (got, far_first, far_second, back_traded, front_traded)
    )
    far_traded = lax.ppermute(far_second, "tm", to_core)
    pcs = lax.all_to_all(sum_for_all(got), BOTH, 0, 0)
    pcs = pcs.reshape(modes // 8, hours // 128, 8, 128)

    pieces = [own, own_traded, from_back, back_traded, from_front, front_traded, far_first, far_traded]
    step = lax.div(band, 2)
    distance = jnp.where(step == 0, 0, jnp.where(step == 1, chips - 1, step - 1))
    places = 2 * lax.rem(chip + distance, chips) + lax.rem(band + core, 2)
    scores = hum_scores(places, pieces)
    return correlate(pcs, scores, mask_float / hours).transpose(0, 2, 1)


def solution(mesh):
    in_specs = (P(None, "space", "tm"), P(None, "space", "tm"), P(), P("tm", "space"))
    out_specs = P("tm", "space", None)
    return jax.shard_map(
        per_device, mesh=mesh, in_specs=in_specs, out_specs=out_specs, check_vma=False
    )
```

```python
import math

import jax
import jax.numpy as jnp
from jax import lax
from jax.experimental import pallas as pl
from jax.experimental.pallas import tpu as pltpu
from jax.sharding import PartitionSpec as P

BOTH = ("tm", "space")
F32 = jnp.float32
BF16 = jnp.bfloat16
EPS = 1e-05
PACK_VMEM = 56 * 1024 * 1024
NT = (((1,), (1,)), ((), ()))
NN = (((1,), (0,)), ((), ()))


def params():
    return pltpu.CompilerParams(vmem_limit_bytes=16 * 1024 * 1024)


def row_chunks(rows, step):
    return [(start, min(step, rows - start)) for start in range(0, rows, step)]


def three_terms(x):
    high = x.astype(BF16)
    rest = x - high.astype(F32)
    middle = rest.astype(BF16)
    low = (rest - middle.astype(F32)).astype(BF16)
    return high, middle, low


def pack_kernel(in_ref, out_ref, held, loaded, stored):
    halves, _, octets, _, _ = in_ref.shape
    places = [(o, h) for o in range(octets) for h in range(halves)]
    loads = [
        pltpu.make_async_copy(in_ref.at[h, :, o], held.at[o, h], loaded.at[n])
        for n, (o, h) in enumerate(places)
    ]
    stores = [
        pltpu.make_async_copy(held.at[o, h], out_ref.at[o, h], stored.at[n])
        for n, (o, h) in enumerate(places)
    ]
    for load in loads:
        load.start()
    for load, store in zip(loads, stores):
        load.wait()
        store.start()
    for store in stores:
        store.wait()


def pack_octets(field):
    halves, lons, octets, rows, width = field.shape
    shape = (octets, halves, lons, rows, width)
    return pl.pallas_call(
        pack_kernel,
        in_specs=[pl.BlockSpec(memory_space=pl.ANY)],
        out_specs=pl.BlockSpec(memory_space=pl.ANY),
        out_shape=jax.ShapeDtypeStruct(shape, field.dtype),
        scratch_shapes=[
            pltpu.VMEM(shape, field.dtype),
            pltpu.SemaphoreType.DMA((octets * halves,)),
            pltpu.SemaphoreType.DMA((octets * halves,)),
        ],
        compiler_params=pltpu.CompilerParams(vmem_limit_bytes=PACK_VMEM),
        cost_estimate=pl.CostEstimate(flops=0, bytes_accessed=4 * field.size, transcendentals=0),
    )(field)


def split_kernel(modes, e_ref, out_ref):
    for n, term in enumerate(three_terms(e_ref[...])):
        out_ref[n * modes : (n + 1) * modes, :] = term


def split_columns(columns_t):
    modes, hours = columns_t.shape
    return pl.pallas_call(
        lambda e_ref, out_ref: split_kernel(modes, e_ref, out_ref),
        out_shape=jax.ShapeDtypeStruct((3 * modes, hours), BF16),
        compiler_params=params(),
        cost_estimate=pl.CostEstimate(flops=0, bytes_accessed=5 * modes * hours * 2, transcendentals=0),
    )(columns_t)


def scores_kernel(t_ref, w_ref, z_ref):
    blocks, cells, width = t_ref.shape
    hours = blocks * width
    weights = jnp.broadcast_to(w_ref[...], (128, cells)).T
    for start, size in row_chunks(cells, 48):
        rows = slice(start, start + size)
        total = jnp.zeros((size, width), F32)
        for b in range(blocks):
            total = total + t_ref[b, rows, :].astype(F32)
        average = jnp.sum(total, axis=1, keepdims=True) / hours
        square = jnp.zeros((size, width), F32)
        for b in range(blocks):
            centered = t_ref[b, rows, :].astype(F32) - average
            square = square + centered * centered
        scale = lax.rsqrt(jnp.sum(square, axis=1, keepdims=True) / hours + EPS)
        weight = weights[rows, :1]
        for b in range(blocks):
            centered = t_ref[b, rows, :].astype(F32) - average
            z_ref[rows, b * width : (b + 1) * width] = ((centered * scale) * weight).astype(BF16)


def sums_kernel(z_ref, e_ref, out_ref):
    modes = out_ref.shape[0]
    loadings = lax.dot_general(z_ref[...], e_ref[...], NT, preferred_element_type=F32)
    turned = loadings.T
    turned = turned[:modes] + (turned[modes : 2 * modes] + turned[2 * modes :])
    stacked = jnp.concatenate(three_terms(turned), axis=0)
    hours = out_ref.shape[1]
    for start, size in row_chunks(hours, 512):
        columns = slice(start, start + size)
        sums = lax.dot_general(stacked, z_ref[:, columns], NN, preferred_element_type=F32)
        out_ref[:, columns] = sums[:modes] + (sums[modes : 2 * modes] + sums[2 * modes :])


def temp_sums(temp, split, weight):
    blocks, cells, width = temp.shape
    modes = split.shape[0] // 3
    scores = pl.pallas_call(
        scores_kernel,
        out_shape=jax.ShapeDtypeStruct((cells, blocks * width), BF16),
        compiler_params=params(),
        cost_estimate=pl.CostEstimate(
            flops=16 * temp.size, bytes_accessed=4 * temp.size, transcendentals=cells
        ),
    )(temp, weight)
    return pl.pallas_call(
        sums_kernel,
        out_shape=jax.ShapeDtypeStruct((modes, blocks * width), F32),
        compiler_params=params(),
        cost_estimate=pl.CostEstimate(
            flops=12 * cells * modes * blocks * width,
            bytes_accessed=2 * temp.size + 2 * split.size,
            transcendentals=0,
        ),
    )(scores, split)


def sum_kernel(got_ref, out_ref):
    count = got_ref.shape[0]
    parts = []
    for n in range(8):
        part = got_ref[n]
        for m in range(n + 8, count, 8):
            part = part + got_ref[m]
        parts.append(part)
    while len(parts) > 1:
        parts = [parts[n] + parts[n + 1] for n in range(0, len(parts), 2)]
    for n in range(count):
        out_ref[n] = parts[0]


def sum_for_all(got):
    return pl.pallas_call(
        sum_kernel,
        out_shape=jax.ShapeDtypeStruct(got.shape, F32),
        compiler_params=params(),
        cost_estimate=pl.CostEstimate(flops=got.size, bytes_accessed=8 * got.size, transcendentals=0),
    )(got)


def band_kernel(place_ref, h_ref, out_ref):
    lons, lats, width = h_ref.shape
    low = lax.broadcasted_iota(jnp.int32, (1, 8, width), 1) < 4
    for start, size in row_chunks(lons, 16):
        for top in range(0, lats, 16):
            tiles = h_ref[start : start + size, top : top + 16, :].astype(F32)
            for q in range(2):
                pairs = tiles[:, 8 * q : 8 * q + 8, :].reshape(size // 2, 2, 8, width)
                even, odd = pairs[:, 0], pairs[:, 1]
                first = jnp.where(low, even, jnp.roll(odd, 4, axis=1))
                second = jnp.where(low, jnp.roll(even, 4, axis=1), odd)
                rows = slice(4 * start, 4 * (start + size))
                band = top // 4 + 2 * q
                out_ref[place_ref[band], rows, :] = first.reshape(4 * size, width).astype(BF16)
                out_ref[place_ref[band + 1], rows, :] = second.reshape(4 * size, width).astype(BF16)


def lay_out_bands(places, hum):
    lons, lats, width = hum.shape
    return pl.pallas_call(
        band_kernel,
        in_specs=[pl.BlockSpec(memory_space=pltpu.SMEM), pl.BlockSpec(memory_space=pltpu.VMEM)],
        out_shape=jax.ShapeDtypeStruct((lats // 4, 4 * lons, width), BF16),
        compiler_params=params(),
        cost_estimate=pl.CostEstimate(flops=0, bytes_accessed=4 * hum.size, transcendentals=0),
    )(places, hum)


def hum_kernel(place_ref, *refs):
    pieces, out_ref = refs[:-1], refs[-1]
    count = len(pieces)
    _, cells, width = pieces[0].shape
    hours = count * width
    for start, size in row_chunks(cells, 48):
        rows = slice(start, start + size)
        total = jnp.zeros((size, width), F32)
        for piece in pieces:
            total = total + piece[0, rows, :].astype(F32)
        average = jnp.sum(total, axis=1, keepdims=True) / hours
        square = jnp.zeros((size, width), F32)
        for piece in pieces:
            centered = piece[0, rows, :].astype(F32) - average
            square = square + centered * centered
        scale = lax.rsqrt(jnp.sum(square, axis=1, keepdims=True) / hours + EPS)
        for n, piece in enumerate(pieces):
            centered = piece[0, rows, :].astype(F32) - average
            columns = pl.ds(pl.multiple_of(place_ref[n] * width, width), width)
            out_ref[rows, columns] = (centered * scale).astype(BF16)


def hum_scores(places, pieces):
    count = len(pieces)
    _, cells, width = pieces[0].shape
    return pl.pallas_call(
        hum_kernel,
        in_specs=[pl.BlockSpec(memory_space=pltpu.SMEM)]
        + [pl.BlockSpec(memory_space=pltpu.VMEM)] * count,
        out_shape=jax.ShapeDtypeStruct((cells, count * width), BF16),
        compiler_params=params(),
        cost_estimate=pl.CostEstimate(
            flops=0, bytes_accessed=16 * cells * width * count, transcendentals=0
        ),
    )(places, *pieces)


def final_kernel(pcs_ref, z_ref, factor_ref, out_ref, rows_ref):
    octets, runs, _, _ = pcs_ref.shape
    lats, modes, lons = out_ref.shape
    hours = runs * 128
    rows = []
    for r in range(octets):
        pcs = jnp.concatenate([pcs_ref[r, c] for c in range(runs)], axis=1)
        centered = pcs - jnp.sum(pcs, axis=1, keepdims=True) / hours
        variance = jnp.sum(centered * centered, axis=1, keepdims=True) / hours
        rows.append(centered * lax.rsqrt(variance + EPS))
    pcz = jnp.concatenate(rows, axis=0).astype(BF16)
    rows_ref[:, :modes] = lax.dot_general(z_ref[...], pcz, NT, preferred_element_type=F32)
    for i in range(lats):
        picked = rows_ref[pl.ds(i, lons, stride=lats), :]
        out_ref[i] = picked.T[:modes] * factor_ref[i : i + 1, :]


def correlate(pcs, scores, factor):
    lats, lons = factor.shape
    modes = pcs.shape[0] * pcs.shape[2]
    return pl.pallas_call(
        final_kernel,
        out_shape=jax.ShapeDtypeStruct((lats, modes, lons), F32),
        scratch_shapes=[pltpu.VMEM((lats * lons, 128), F32)],
        compiler_params=params(),
        cost_estimate=pl.CostEstimate(
            flops=2 * scores.size * modes, bytes_accessed=4 * pcs.size + 2 * scores.size, transcendentals=0
        ),
    )(pcs, scores, factor)


def area_root(rows, total_lat):
    latitude = ((rows.astype(F32) + 0.5) / total_lat * 120.0 - 60.0) * (math.pi / 180.0)
    return jnp.sqrt(jnp.cos(latitude))


def per_device(thermal_reading, moisture_content, gram_eigenvector_columns, marine_indicator):
    total_lat, lons, width = thermal_reading.shape
    lats = marine_indicator.shape[0]
    hours, modes = gram_eigenvector_columns.shape
    members = lax.axis_size("tm")
    chips = members // 2
    me = lax.axis_index("tm")
    chip, core = lax.div(me, 2), lax.rem(me, 2)
    to_core = [(n, n ^ 1) for n in range(members)]
    to_chip = [[(n, (n + 2 * d) % members) for n in range(members)] for d in range(chips)]
    mask_float = marine_indicator.astype(F32)

    half = lons // 2
    temp = thermal_reading.transpose(1, 0, 2).reshape(2, half, chips, 8, width)
    temp = pack_octets(temp).reshape(members, 8 * half, width)
    temp = lax.all_to_all(temp, "tm", 0, 0)

    band = jnp.arange(members, dtype=jnp.int32)
    far = lax.rem(lax.div(band, 2) + 2 * chips - chip - 1, chips)
    order = 2 * far + lax.rem(band + core, 2)
    laid = lay_out_bands(order, moisture_content.transpose(1, 0, 2))
    sent, own = [laid[2 * d : 2 * d + 2] for d in range(chips - 1)], laid[2 * chips - 2 :]

    other = lax.ppermute(marine_indicator, "tm", to_core)
    pair = jnp.where(core == 0, jnp.stack([marine_indicator, other]), jnp.stack([other, marine_indicator]))
    pair, *sent = lax.optimization_barrier((pair, *sent))
    arrived = [lax.ppermute(sent[d - 1], "tm", to_chip[d]) for d in range(1, chips)]
    root = area_root(8 * chip + jnp.arange(8, dtype=jnp.int32), total_lat)
    scaling = root[:, None] * pair.reshape(8, lons).astype(F32)
    weight = lax.dynamic_slice(scaling.T, (core * half, 0), (half, 8)).reshape(1, 8 * half)

    partial_t = temp_sums(temp, split_columns(gram_eigenvector_columns.T), weight)
    blocks = partial_t.reshape(modes // 8, 8, hours // 128, 128)
    blocks = blocks.transpose(0, 2, 1, 3).reshape(-1, 8, 128)
    got = lax.all_to_all(blocks, BOTH, 0, 0)
    traded = [lax.ppermute(blocks[1:2], "tm", to_core) for blocks in [own, *arrived]]
    got, *traded = lax.optimization_barrier((got, *traded))
    pcs = lax.all_to_all(sum_for_all(got), BOTH, 0, 0)
    pcs = pcs.reshape(modes // 8, hours // 128, 8, 128)

    pieces = [piece for both in zip([own, *arrived], traded) for piece in both]
    places = 2 * lax.rem(chip + chips - lax.div(band, 2), chips) + lax.rem(band + core, 2)
    scores = hum_scores(places, pieces)
    return correlate(pcs, scores, mask_float / hours).transpose(0, 2, 1)


def solution(mesh):
    in_specs = (P(None, "space", "tm"), P(None, "space", "tm"), P(), P("tm", "space"))
    out_specs = P("tm", "space", None)
    return jax.shard_map(
        per_device, mesh=mesh, in_specs=in_specs, out_specs=out_specs, check_vma=False
    )
```

```python
import math

import jax
import jax.numpy as jnp
from jax import lax
from jax.experimental import pallas as pl
from jax.experimental.pallas import tpu as pltpu
from jax.sharding import PartitionSpec as P

BOTH = ("tm", "space")
F32 = jnp.float32
BF16 = jnp.bfloat16
EPS = 1e-05
PACK_VMEM = 56 * 1024 * 1024
PARTS = 3
NT = (((1,), (1,)), ((), ()))
NN = (((1,), (0,)), ((), ()))


def params():
    return pltpu.CompilerParams(vmem_limit_bytes=16 * 1024 * 1024)


def row_chunks(rows, step):
    return [(start, min(step, rows - start)) for start in range(0, rows, step)]


def three_terms(x):
    high = x.astype(BF16)
    rest = x - high.astype(F32)
    middle = rest.astype(BF16)
    low = (rest - middle.astype(F32)).astype(BF16)
    return high, middle, low


def pack_kernel(in_ref, out_ref, held, loaded, stored):
    halves, lons, octets, _, _ = in_ref.shape
    part = lons // PARTS
    places = [
        (o, h, slice(p * part, (p + 1) * part if p < PARTS - 1 else lons))
        for o in range(octets)
        for h in range(halves)
        for p in range(PARTS)
    ]
    loads = [
        pltpu.make_async_copy(in_ref.at[h, run, o], held.at[o, h, run], loaded.at[n])
        for n, (o, h, run) in enumerate(places)
    ]
    stores = [
        pltpu.make_async_copy(held.at[o, h, run], out_ref.at[o, h, run], stored.at[n])
        for n, (o, h, run) in enumerate(places)
    ]
    for load in loads:
        load.start()
    for load, store in zip(loads, stores):
        load.wait()
        store.start()
    for store in stores:
        store.wait()


def pack_octets(field):
    halves, lons, octets, rows, width = field.shape
    shape = (octets, halves, lons, rows, width)
    return pl.pallas_call(
        pack_kernel,
        in_specs=[pl.BlockSpec(memory_space=pl.ANY)],
        out_specs=pl.BlockSpec(memory_space=pl.ANY),
        out_shape=jax.ShapeDtypeStruct(shape, field.dtype),
        scratch_shapes=[
            pltpu.VMEM(shape, field.dtype),
            pltpu.SemaphoreType.DMA((octets * halves * PARTS,)),
            pltpu.SemaphoreType.DMA((octets * halves * PARTS,)),
        ],
        compiler_params=pltpu.CompilerParams(vmem_limit_bytes=PACK_VMEM),
        cost_estimate=pl.CostEstimate(flops=0, bytes_accessed=4 * field.size, transcendentals=0),
    )(field)


def split_kernel(modes, e_ref, out_ref):
    for n, term in enumerate(three_terms(e_ref[...])):
        out_ref[n * modes : (n + 1) * modes, :] = term


def split_columns(columns_t):
    modes, hours = columns_t.shape
    return pl.pallas_call(
        lambda e_ref, out_ref: split_kernel(modes, e_ref, out_ref),
        out_shape=jax.ShapeDtypeStruct((3 * modes, hours), BF16),
        compiler_params=params(),
        cost_estimate=pl.CostEstimate(flops=0, bytes_accessed=5 * modes * hours * 2, transcendentals=0),
    )(columns_t)


def scores_kernel(t_ref, w_ref, z_ref):
    blocks, cells, width = t_ref.shape
    hours = blocks * width
    weights = jnp.broadcast_to(w_ref[...], (128, cells)).T
    for start, size in row_chunks(cells, 48):
        rows = slice(start, start + size)
        total = jnp.zeros((size, width), F32)
        for b in range(blocks):
            total = total + t_ref[b, rows, :].astype(F32)
        average = jnp.sum(total, axis=1, keepdims=True) / hours
        square = jnp.zeros((size, width), F32)
        for b in range(blocks):
            centered = t_ref[b, rows, :].astype(F32) - average
            square = square + centered * centered
        scale = lax.rsqrt(jnp.sum(square, axis=1, keepdims=True) / hours + EPS)
        weight = weights[rows, :1]
        for b in range(blocks):
            centered = t_ref[b, rows, :].astype(F32) - average
            z_ref[rows, b * width : (b + 1) * width] = ((centered * scale) * weight).astype(BF16)


def sums_kernel(z_ref, e_ref, out_ref):
    modes = out_ref.shape[0]
    turned = lax.dot_general(e_ref[...], z_ref[...], NT, preferred_element_type=F32)
    turned = turned[:modes] + (turned[modes : 2 * modes] + turned[2 * modes :])
    stacked = jnp.concatenate(three_terms(turned), axis=0)
    hours = out_ref.shape[1]
    for start, size in row_chunks(hours, 512):
        columns = slice(start, start + size)
        sums = lax.dot_general(stacked, z_ref[:, columns], NN, preferred_element_type=F32)
        out_ref[:, columns] = sums[:modes] + (sums[modes : 2 * modes] + sums[2 * modes :])


def temp_sums(temp, split, weight):
    blocks, cells, width = temp.shape
    modes = split.shape[0] // 3
    scores = pl.pallas_call(
        scores_kernel,
        out_shape=jax.ShapeDtypeStruct((cells, blocks * width), BF16),
        compiler_params=params(),
        cost_estimate=pl.CostEstimate(
            flops=16 * temp.size, bytes_accessed=4 * temp.size, transcendentals=cells
        ),
    )(temp, weight)
    return pl.pallas_call(
        sums_kernel,
        out_shape=jax.ShapeDtypeStruct((modes, blocks * width), F32),
        compiler_params=params(),
        cost_estimate=pl.CostEstimate(
            flops=12 * cells * modes * blocks * width,
            bytes_accessed=2 * temp.size + 2 * split.size,
            transcendentals=0,
        ),
    )(scores, split)


def sum_kernel(got_ref, out_ref):
    count = got_ref.shape[0]
    parts = []
    for n in range(8):
        part = got_ref[n]
        for m in range(n + 8, count, 8):
            part = part + got_ref[m]
        parts.append(part)
    while len(parts) > 1:
        parts = [parts[n] + parts[n + 1] for n in range(0, len(parts), 2)]
    for n in range(count):
        out_ref[n] = parts[0]


def sum_for_all(got):
    return pl.pallas_call(
        sum_kernel,
        out_shape=jax.ShapeDtypeStruct(got.shape, F32),
        compiler_params=params(),
        cost_estimate=pl.CostEstimate(flops=got.size, bytes_accessed=8 * got.size, transcendentals=0),
    )(got)


def band_kernel(place_ref, h_ref, out_ref):
    lons, lats, width = h_ref.shape
    low = lax.broadcasted_iota(jnp.int32, (1, 8, width), 1) < 4
    for start, size in row_chunks(lons, 16):
        for top in range(0, lats, 16):
            tiles = h_ref[start : start + size, top : top + 16, :].astype(F32)
            for q in range(2):
                pairs = tiles[:, 8 * q : 8 * q + 8, :].reshape(size // 2, 2, 8, width)
                even, odd = pairs[:, 0], pairs[:, 1]
                first = jnp.where(low, even, jnp.roll(odd, 4, axis=1))
                second = jnp.where(low, jnp.roll(even, 4, axis=1), odd)
                rows = slice(4 * start, 4 * (start + size))
                band = top // 4 + 2 * q
                out_ref[place_ref[band], rows, :] = first.reshape(4 * size, width).astype(BF16)
                out_ref[place_ref[band + 1], rows, :] = second.reshape(4 * size, width).astype(BF16)


def lay_out_bands(places, hum):
    lons, lats, width = hum.shape
    return pl.pallas_call(
        band_kernel,
        in_specs=[pl.BlockSpec(memory_space=pltpu.SMEM), pl.BlockSpec(memory_space=pltpu.VMEM)],
        out_shape=jax.ShapeDtypeStruct((lats // 4, 4 * lons, width), BF16),
        compiler_params=params(),
        cost_estimate=pl.CostEstimate(flops=0, bytes_accessed=4 * hum.size, transcendentals=0),
    )(places, hum)


def hum_kernel(place_ref, *refs):
    pieces, out_ref = refs[:-1], refs[-1]
    count = len(pieces)
    _, cells, width = pieces[0].shape
    hours = count * width
    for start, size in row_chunks(cells, 48):
        rows = slice(start, start + size)
        total = jnp.zeros((size, width), F32)
        for piece in pieces:
            total = total + piece[0, rows, :].astype(F32)
        average = jnp.sum(total, axis=1, keepdims=True) / hours
        square = jnp.zeros((size, width), F32)
        for piece in pieces:
            centered = piece[0, rows, :].astype(F32) - average
            square = square + centered * centered
        scale = lax.rsqrt(jnp.sum(square, axis=1, keepdims=True) / hours + EPS)
        for n, piece in enumerate(pieces):
            centered = piece[0, rows, :].astype(F32) - average
            columns = pl.ds(pl.multiple_of(place_ref[n] * width, width), width)
            out_ref[rows, columns] = (centered * scale).astype(BF16)


def hum_scores(places, pieces):
    count = len(pieces)
    _, cells, width = pieces[0].shape
    return pl.pallas_call(
        hum_kernel,
        in_specs=[pl.BlockSpec(memory_space=pltpu.SMEM)]
        + [pl.BlockSpec(memory_space=pltpu.VMEM)] * count,
        out_shape=jax.ShapeDtypeStruct((cells, count * width), BF16),
        compiler_params=params(),
        cost_estimate=pl.CostEstimate(
            flops=0, bytes_accessed=16 * cells * width * count, transcendentals=0
        ),
    )(places, *pieces)


def final_kernel(pcs_ref, z_ref, factor_ref, out_ref, rows_ref):
    octets, runs, _, _ = pcs_ref.shape
    lats, modes, lons = out_ref.shape
    hours = runs * 128
    rows = []
    for r in range(octets):
        pcs = jnp.concatenate([pcs_ref[r, c] for c in range(runs)], axis=1)
        centered = pcs - jnp.sum(pcs, axis=1, keepdims=True) / hours
        variance = jnp.sum(centered * centered, axis=1, keepdims=True) / hours
        rows.append(centered * lax.rsqrt(variance + EPS))
    pcz = jnp.concatenate(rows, axis=0).astype(BF16)
    rows_ref[:, :modes] = lax.dot_general(z_ref[...], pcz, NT, preferred_element_type=F32)
    for i in range(lats):
        picked = rows_ref[pl.ds(i, lons, stride=lats), :]
        out_ref[i] = picked.T[:modes] * factor_ref[i : i + 1, :]


def correlate(pcs, scores, factor):
    lats, lons = factor.shape
    modes = pcs.shape[0] * pcs.shape[2]
    return pl.pallas_call(
        final_kernel,
        out_shape=jax.ShapeDtypeStruct((lats, modes, lons), F32),
        scratch_shapes=[pltpu.VMEM((lats * lons, 128), F32)],
        compiler_params=params(),
        cost_estimate=pl.CostEstimate(
            flops=2 * scores.size * modes, bytes_accessed=4 * pcs.size + 2 * scores.size, transcendentals=0
        ),
    )(pcs, scores, factor)


def area_root(rows, total_lat):
    latitude = ((rows.astype(F32) + 0.5) / total_lat * 120.0 - 60.0) * (math.pi / 180.0)
    return jnp.sqrt(jnp.cos(latitude))


def per_device(thermal_reading, moisture_content, gram_eigenvector_columns, marine_indicator):
    total_lat, lons, width = thermal_reading.shape
    lats = marine_indicator.shape[0]
    hours, modes = gram_eigenvector_columns.shape
    members = lax.axis_size("tm")
    chips = members // 2
    me = lax.axis_index("tm")
    chip, core = lax.div(me, 2), lax.rem(me, 2)
    to_core = [(n, n ^ 1) for n in range(members)]
    to_chip = [[(n, (n + 2 * d) % members) for n in range(members)] for d in range(chips)]
    mask_float = marine_indicator.astype(F32)

    half = lons // 2
    temp = thermal_reading.transpose(1, 0, 2).reshape(2, half, chips, 8, width)
    temp = pack_octets(temp).reshape(members, 8 * half, width)
    temp = lax.all_to_all(temp, "tm", 0, 0)

    band = jnp.arange(members, dtype=jnp.int32)
    far = lax.rem(lax.div(band, 2) + 2 * chips - chip - 1, chips)
    order = 2 * far + lax.rem(band + core, 2)
    laid = lay_out_bands(order, moisture_content.transpose(1, 0, 2))
    sent, own = [laid[2 * d : 2 * d + 2] for d in range(chips - 1)], laid[2 * chips - 2 :]

    other = lax.ppermute(marine_indicator, "tm", to_core)
    pair = jnp.where(core == 0, jnp.stack([marine_indicator, other]), jnp.stack([other, marine_indicator]))
    pair, *sent = lax.optimization_barrier((pair, *sent))
    arrived = [lax.ppermute(sent[d - 1], "tm", to_chip[d]) for d in range(1, chips)]
    root = area_root(8 * chip + jnp.arange(8, dtype=jnp.int32), total_lat)
    scaling = root[:, None] * pair.reshape(8, lons).astype(F32)
    weight = lax.dynamic_slice(scaling.T, (core * half, 0), (half, 8)).reshape(1, 8 * half)

    partial_t = temp_sums(temp, split_columns(gram_eigenvector_columns.T), weight)
    blocks = partial_t.reshape(modes // 8, 8, hours // 128, 128)
    blocks = blocks.transpose(0, 2, 1, 3).reshape(-1, 8, 128)
    got = lax.all_to_all(blocks, BOTH, 0, 0)
    traded = [lax.ppermute(blocks[1:2], "tm", to_core) for blocks in [own, *arrived]]
    got, *traded = lax.optimization_barrier((got, *traded))
    pcs = lax.all_to_all(sum_for_all(got), BOTH, 0, 0)
    pcs = pcs.reshape(modes // 8, hours // 128, 8, 128)

    pieces = [piece for both in zip([own, *arrived], traded) for piece in both]
    places = 2 * lax.rem(chip + chips - lax.div(band, 2), chips) + lax.rem(band + core, 2)
    scores = hum_scores(places, pieces)
    return correlate(pcs, scores, mask_float / hours).transpose(0, 2, 1)


def solution(mesh):
    in_specs = (P(None, "space", "tm"), P(None, "space", "tm"), P(), P("tm", "space"))
    out_specs = P("tm", "space", None)
    return jax.shard_map(
        per_device, mesh=mesh, in_specs=in_specs, out_specs=out_specs, check_vma=False
    )
```

```python
import math

import jax
import jax.numpy as jnp
from jax import lax
from jax.experimental import pallas as pl
from jax.experimental.pallas import tpu as pltpu
from jax.sharding import PartitionSpec as P

BOTH = ("tm", "space")
F32 = jnp.float32
BF16 = jnp.bfloat16
EPS = 1e-05
PACK_VMEM = 56 * 1024 * 1024
PARTS = 3
NT = (((1,), (1,)), ((), ()))
NN = (((1,), (0,)), ((), ()))


def params():
    return pltpu.CompilerParams(vmem_limit_bytes=16 * 1024 * 1024)


def row_chunks(rows, step):
    return [(start, min(step, rows - start)) for start in range(0, rows, step)]


def three_terms(x):
    high = x.astype(BF16)
    rest = x - high.astype(F32)
    middle = rest.astype(BF16)
    low = (rest - middle.astype(F32)).astype(BF16)
    return high, middle, low


def pack_kernel(in_ref, out_ref, held, loaded, stored):
    halves, lons, octets, _, _ = in_ref.shape
    part = lons // PARTS
    places = [
        (o, h, slice(p * part, (p + 1) * part if p < PARTS - 1 else lons))
        for o in range(octets)
        for h in range(halves)
        for p in range(PARTS)
    ]
    loads = [
        pltpu.make_async_copy(in_ref.at[h, run, o], held.at[o, h, run], loaded.at[n])
        for n, (o, h, run) in enumerate(places)
    ]
    stores = [
        pltpu.make_async_copy(held.at[o, h, run], out_ref.at[o, h, run], stored.at[n])
        for n, (o, h, run) in enumerate(places)
    ]
    for load in loads:
        load.start()
    for load, store in zip(loads, stores):
        load.wait()
        store.start()
    for store in stores:
        store.wait()


def pack_octets(field):
    halves, lons, octets, rows, width = field.shape
    shape = (octets, halves, lons, rows, width)
    return pl.pallas_call(
        pack_kernel,
        in_specs=[pl.BlockSpec(memory_space=pl.ANY)],
        out_specs=pl.BlockSpec(memory_space=pl.ANY),
        out_shape=jax.ShapeDtypeStruct(shape, field.dtype),
        scratch_shapes=[
            pltpu.VMEM(shape, field.dtype),
            pltpu.SemaphoreType.DMA((octets * halves * PARTS,)),
            pltpu.SemaphoreType.DMA((octets * halves * PARTS,)),
        ],
        compiler_params=pltpu.CompilerParams(vmem_limit_bytes=PACK_VMEM),
        cost_estimate=pl.CostEstimate(flops=0, bytes_accessed=4 * field.size, transcendentals=0),
    )(field)


def split_kernel(modes, e_ref, out_ref):
    for n, term in enumerate(three_terms(e_ref[...])):
        out_ref[n * modes : (n + 1) * modes, :] = term


def split_columns(columns_t):
    modes, hours = columns_t.shape
    return pl.pallas_call(
        lambda e_ref, out_ref: split_kernel(modes, e_ref, out_ref),
        out_shape=jax.ShapeDtypeStruct((3 * modes, hours), BF16),
        compiler_params=params(),
        cost_estimate=pl.CostEstimate(flops=0, bytes_accessed=5 * modes * hours * 2, transcendentals=0),
    )(columns_t)


def scores_kernel(t_ref, w_ref, z_ref):
    blocks, cells, width = t_ref.shape
    hours = blocks * width
    weights = jnp.broadcast_to(w_ref[...], (128, cells)).T
    for start, size in row_chunks(cells, 48):
        rows = slice(start, start + size)
        total = jnp.zeros((size, width), F32)
        for b in range(blocks):
            total = total + t_ref[b, rows, :].astype(F32)
        average = jnp.sum(total, axis=1, keepdims=True) / hours
        square = jnp.zeros((size, width), F32)
        for b in range(blocks):
            centered = t_ref[b, rows, :].astype(F32) - average
            square = square + centered * centered
        scale = lax.rsqrt(jnp.sum(square, axis=1, keepdims=True) / hours + EPS)
        weight = weights[rows, :1]
        for b in range(blocks):
            centered = t_ref[b, rows, :].astype(F32) - average
            z_ref[rows, b * width : (b + 1) * width] = ((centered * scale) * weight).astype(BF16)


def sums_kernel(z_ref, e_ref, out_ref):
    modes = out_ref.shape[0]
    turned = lax.dot_general(e_ref[...], z_ref[...], NT, preferred_element_type=F32)
    turned = turned[:modes] + (turned[modes : 2 * modes] + turned[2 * modes :])
    stacked = jnp.concatenate(three_terms(turned), axis=0)
    hours = out_ref.shape[1]
    for start, size in row_chunks(hours, 512):
        columns = slice(start, start + size)
        sums = lax.dot_general(stacked, z_ref[:, columns], NN, preferred_element_type=F32)
        out_ref[:, columns] = sums[:modes] + (sums[modes : 2 * modes] + sums[2 * modes :])


def temp_sums(temp, split, weight):
    blocks, cells, width = temp.shape
    modes = split.shape[0] // 3
    scores = pl.pallas_call(
        scores_kernel,
        out_shape=jax.ShapeDtypeStruct((cells, blocks * width), BF16),
        compiler_params=params(),
        cost_estimate=pl.CostEstimate(
            flops=16 * temp.size, bytes_accessed=4 * temp.size, transcendentals=cells
        ),
    )(temp, weight)
    return pl.pallas_call(
        sums_kernel,
        out_shape=jax.ShapeDtypeStruct((modes, blocks * width), F32),
        compiler_params=params(),
        cost_estimate=pl.CostEstimate(
            flops=12 * cells * modes * blocks * width,
            bytes_accessed=2 * temp.size + 2 * split.size,
            transcendentals=0,
        ),
    )(scores, split)


def sum_kernel(got_ref, out_ref):
    count = got_ref.shape[0]
    parts = []
    for n in range(8):
        part = got_ref[n]
        for m in range(n + 8, count, 8):
            part = part + got_ref[m]
        parts.append(part)
    while len(parts) > 1:
        parts = [parts[n] + parts[n + 1] for n in range(0, len(parts), 2)]
    for n in range(out_ref.shape[0]):
        out_ref[n] = parts[0]


def sum_for_all(got, copies):
    return pl.pallas_call(
        sum_kernel,
        out_shape=jax.ShapeDtypeStruct((copies, *got.shape[1:]), F32),
        compiler_params=params(),
        cost_estimate=pl.CostEstimate(flops=got.size, bytes_accessed=8 * got.size, transcendentals=0),
    )(got)


def band_kernel(place_ref, h_ref, out_ref):
    lons, lats, width = h_ref.shape
    low = lax.broadcasted_iota(jnp.int32, (1, 8, width), 1) < 4
    for start, size in row_chunks(lons, 16):
        for top in range(0, lats, 16):
            tiles = h_ref[start : start + size, top : top + 16, :].astype(F32)
            for q in range(2):
                pairs = tiles[:, 8 * q : 8 * q + 8, :].reshape(size // 2, 2, 8, width)
                even, odd = pairs[:, 0], pairs[:, 1]
                first = jnp.where(low, even, jnp.roll(odd, 4, axis=1))
                second = jnp.where(low, jnp.roll(even, 4, axis=1), odd)
                rows = slice(4 * start, 4 * (start + size))
                band = top // 4 + 2 * q
                out_ref[place_ref[band], rows, :] = first.reshape(4 * size, width).astype(BF16)
                out_ref[place_ref[band + 1], rows, :] = second.reshape(4 * size, width).astype(BF16)


def lay_out_bands(places, hum):
    lons, lats, width = hum.shape
    return pl.pallas_call(
        band_kernel,
        in_specs=[pl.BlockSpec(memory_space=pltpu.SMEM), pl.BlockSpec(memory_space=pltpu.VMEM)],
        out_shape=jax.ShapeDtypeStruct((lats // 4, 4 * lons, width), BF16),
        compiler_params=params(),
        cost_estimate=pl.CostEstimate(flops=0, bytes_accessed=4 * hum.size, transcendentals=0),
    )(places, hum)


def hum_kernel(place_ref, *refs):
    pieces, out_ref = refs[:-1], refs[-1]
    count = len(pieces)
    _, cells, width = pieces[0].shape
    hours = count * width
    for start, size in row_chunks(cells, 48):
        rows = slice(start, start + size)
        total = jnp.zeros((size, width), F32)
        for piece in pieces:
            total = total + piece[0, rows, :].astype(F32)
        average = jnp.sum(total, axis=1, keepdims=True) / hours
        square = jnp.zeros((size, width), F32)
        for piece in pieces:
            centered = piece[0, rows, :].astype(F32) - average
            square = square + centered * centered
        scale = lax.rsqrt(jnp.sum(square, axis=1, keepdims=True) / hours + EPS)
        for n, piece in enumerate(pieces):
            centered = piece[0, rows, :].astype(F32) - average
            columns = pl.ds(pl.multiple_of(place_ref[n] * width, width), width)
            out_ref[rows, columns] = (centered * scale).astype(BF16)


def hum_scores(places, pieces):
    count = len(pieces)
    _, cells, width = pieces[0].shape
    return pl.pallas_call(
        hum_kernel,
        in_specs=[pl.BlockSpec(memory_space=pltpu.SMEM)]
        + [pl.BlockSpec(memory_space=pltpu.VMEM)] * count,
        out_shape=jax.ShapeDtypeStruct((cells, count * width), BF16),
        compiler_params=params(),
        cost_estimate=pl.CostEstimate(
            flops=0, bytes_accessed=16 * cells * width * count, transcendentals=0
        ),
    )(places, *pieces)


def final_kernel(core_ref, own_ref, other_ref, z_ref, factor_ref, out_ref, rows_ref):
    octets, runs, _, _ = own_ref.shape
    core = core_ref[0]
    lats, modes, lons = out_ref.shape
    hours = runs * 128
    rows = []
    for r in range(2 * octets):
        own = jnp.concatenate([own_ref[r // 2, c] for c in range(runs)], axis=1)
        other = jnp.concatenate([other_ref[r // 2, c] for c in range(runs)], axis=1)
        pcs = jnp.where(core == r % 2, own, other)
        centered = pcs - jnp.sum(pcs, axis=1, keepdims=True) / hours
        variance = jnp.sum(centered * centered, axis=1, keepdims=True) / hours
        rows.append(centered * lax.rsqrt(variance + EPS))
    pcz = jnp.concatenate(rows, axis=0).astype(BF16)
    rows_ref[:, :modes] = lax.dot_general(z_ref[...], pcz, NT, preferred_element_type=F32)
    for i in range(lats):
        picked = rows_ref[pl.ds(i, lons, stride=lats), :]
        out_ref[i] = picked.T[:modes] * factor_ref[i : i + 1, :]


def correlate(core, own, other, scores, factor):
    lats, lons = factor.shape
    modes = 2 * own.shape[0] * own.shape[2]
    vmem = pl.BlockSpec(memory_space=pltpu.VMEM)
    return pl.pallas_call(
        final_kernel,
        in_specs=[pl.BlockSpec(memory_space=pltpu.SMEM), vmem, vmem, vmem, vmem],
        out_shape=jax.ShapeDtypeStruct((lats, modes, lons), F32),
        scratch_shapes=[pltpu.VMEM((lats * lons, 128), F32)],
        compiler_params=params(),
        cost_estimate=pl.CostEstimate(
            flops=2 * scores.size * modes, bytes_accessed=8 * own.size + 2 * scores.size, transcendentals=0
        ),
    )(core.reshape(1), own, other, scores, factor)


def area_root(rows, total_lat):
    latitude = ((rows.astype(F32) + 0.5) / total_lat * 120.0 - 60.0) * (math.pi / 180.0)
    return jnp.sqrt(jnp.cos(latitude))


def per_device(thermal_reading, moisture_content, gram_eigenvector_columns, marine_indicator):
    total_lat, lons, width = thermal_reading.shape
    lats = marine_indicator.shape[0]
    hours, modes = gram_eigenvector_columns.shape
    members = lax.axis_size("tm")
    others = lax.axis_size("space")
    chips = members // 2
    me = lax.axis_index("tm")
    chip, core = lax.div(me, 2), lax.rem(me, 2)
    to_core = [(n, n ^ 1) for n in range(members)]
    to_chip = [[(n, (n + 2 * d) % members) for n in range(members)] for d in range(chips)]
    mask_float = marine_indicator.astype(F32)

    half = lons // 2
    temp = thermal_reading.transpose(1, 0, 2).reshape(2, half, chips, 8, width)
    temp = pack_octets(temp).reshape(members, 8 * half, width)
    temp = lax.all_to_all(temp, "tm", 0, 0)

    band = jnp.arange(members, dtype=jnp.int32)
    far = lax.rem(lax.div(band, 2) + 2 * chips - chip - 1, chips)
    order = 2 * far + lax.rem(band + core, 2)
    laid = lay_out_bands(order, moisture_content.transpose(1, 0, 2))
    sent, own = [laid[2 * d : 2 * d + 2] for d in range(chips - 1)], laid[2 * chips - 2 :]

    other = lax.ppermute(marine_indicator, "tm", to_core)
    pair = jnp.where(core == 0, jnp.stack([marine_indicator, other]), jnp.stack([other, marine_indicator]))
    pair, *sent = lax.optimization_barrier((pair, *sent))
    arrived = [lax.ppermute(sent[d - 1], "tm", to_chip[d]) for d in range(1, chips)]
    root = area_root(8 * chip + jnp.arange(8, dtype=jnp.int32), total_lat)
    scaling = root[:, None] * pair.reshape(8, lons).astype(F32)
    weight = lax.dynamic_slice(scaling.T, (core * half, 0), (half, 8)).reshape(1, 8 * half)

    partial_t = temp_sums(temp, split_columns(gram_eigenvector_columns.T), weight)
    blocks = partial_t.reshape(modes // 8, 8, hours // 128, 128)
    blocks = blocks.transpose(0, 2, 1, 3).reshape(-1, 8, 128)
    got = lax.all_to_all(blocks, BOTH, 0, 0)
    traded = [lax.ppermute(blocks[1:2], "tm", to_core) for blocks in [own, *arrived]]
    got, *traded = lax.optimization_barrier((got, *traded))
    kinds = [
        [t * others + n for t in range(kind, members, 2) for n in range(others)] for kind in range(2)
    ]
    pcs = lax.all_to_all(sum_for_all(got, chips * others), BOTH, 0, 0, axis_index_groups=kinds)
    pcs = pcs.reshape(chips, others, 8, 128)
    pcs_other = lax.ppermute(pcs, "tm", to_core)

    pieces = [piece for both in zip([own, *arrived], traded) for piece in both]
    places = 2 * lax.rem(chip + chips - lax.div(band, 2), chips) + lax.rem(band + core, 2)
    scores = hum_scores(places, pieces)
    return correlate(core, pcs, pcs_other, scores, mask_float / hours).transpose(0, 2, 1)


def solution(mesh):
    in_specs = (P(None, "space", "tm"), P(None, "space", "tm"), P(), P("tm", "space"))
    out_specs = P("tm", "space", None)
    return jax.shard_map(
        per_device, mesh=mesh, in_specs=in_specs, out_specs=out_specs, check_vma=False
    )
```

```python
import math

import jax
import jax.numpy as jnp
from jax import lax
from jax.experimental import pallas as pl
from jax.experimental.pallas import tpu as pltpu
from jax.sharding import PartitionSpec as P

BOTH = ("tm", "space")
F32 = jnp.float32
BF16 = jnp.bfloat16
EPS = 1e-05
PACK_VMEM = 56 * 1024 * 1024
PARTS = 3
NT = (((1,), (1,)), ((), ()))
NN = (((1,), (0,)), ((), ()))


def params():
    return pltpu.CompilerParams(vmem_limit_bytes=16 * 1024 * 1024)


def row_chunks(rows, step):
    return [(start, min(step, rows - start)) for start in range(0, rows, step)]


def three_terms(x):
    high = x.astype(BF16)
    rest = x - high.astype(F32)
    middle = rest.astype(BF16)
    low = (rest - middle.astype(F32)).astype(BF16)
    return high, middle, low


def pack_kernel(in_ref, out_ref, held, loaded, stored):
    halves, lons, octets, _, _ = in_ref.shape
    part = lons // PARTS
    places = [
        (o, h, slice(p * part, (p + 1) * part if p < PARTS - 1 else lons))
        for o in range(octets)
        for h in range(halves)
        for p in range(PARTS)
    ]
    loads = [
        pltpu.make_async_copy(in_ref.at[h, run, o], held.at[o, h, run], loaded.at[n])
        for n, (o, h, run) in enumerate(places)
    ]
    stores = [
        pltpu.make_async_copy(held.at[o, h, run], out_ref.at[o, h, run], stored.at[n])
        for n, (o, h, run) in enumerate(places)
    ]
    for load in loads:
        load.start()
    for load, store in zip(loads, stores):
        load.wait()
        store.start()
    for store in stores:
        store.wait()


def pack_octets(field):
    halves, lons, octets, rows, width = field.shape
    shape = (octets, halves, lons, rows, width)
    return pl.pallas_call(
        pack_kernel,
        in_specs=[pl.BlockSpec(memory_space=pl.ANY)],
        out_specs=pl.BlockSpec(memory_space=pl.ANY),
        out_shape=jax.ShapeDtypeStruct(shape, field.dtype),
        scratch_shapes=[
            pltpu.VMEM(shape, field.dtype),
            pltpu.SemaphoreType.DMA((octets * halves * PARTS,)),
            pltpu.SemaphoreType.DMA((octets * halves * PARTS,)),
        ],
        compiler_params=pltpu.CompilerParams(vmem_limit_bytes=PACK_VMEM),
        cost_estimate=pl.CostEstimate(flops=0, bytes_accessed=4 * field.size, transcendentals=0),
    )(field)


def split_kernel(modes, e_ref, out_ref):
    for n, term in enumerate(three_terms(e_ref[...])):
        out_ref[n * modes : (n + 1) * modes, :] = term


def split_columns(columns_t):
    modes, hours = columns_t.shape
    return pl.pallas_call(
        lambda e_ref, out_ref: split_kernel(modes, e_ref, out_ref),
        out_shape=jax.ShapeDtypeStruct((3 * modes, hours), BF16),
        compiler_params=params(),
        cost_estimate=pl.CostEstimate(flops=0, bytes_accessed=5 * modes * hours * 2, transcendentals=0),
    )(columns_t)


def scores_kernel(t_ref, w_ref, z_ref):
    blocks, cells, width = t_ref.shape
    hours = blocks * width
    weights = jnp.broadcast_to(w_ref[...], (128, cells)).T
    for start, size in row_chunks(cells, 48):
        rows = slice(start, start + size)
        total = jnp.zeros((size, width), F32)
        for b in range(blocks):
            total = total + t_ref[b, rows, :].astype(F32)
        average = jnp.sum(total, axis=1, keepdims=True) / hours
        square = jnp.zeros((size, width), F32)
        for b in range(blocks):
            centered = t_ref[b, rows, :].astype(F32) - average
            square = square + centered * centered
        scale = lax.rsqrt(jnp.sum(square, axis=1, keepdims=True) / hours + EPS)
        weight = weights[rows, :1]
        for b in range(blocks):
            centered = t_ref[b, rows, :].astype(F32) - average
            z_ref[rows, b * width : (b + 1) * width] = ((centered * scale) * weight).astype(BF16)


def sums_kernel(z_ref, e_ref, out_ref):
    modes = out_ref.shape[0]
    turned = lax.dot_general(e_ref[...], z_ref[...], NT, preferred_element_type=F32)
    turned = turned[:modes] + (turned[modes : 2 * modes] + turned[2 * modes :])
    stacked = jnp.concatenate(three_terms(turned), axis=0)
    hours = out_ref.shape[1]
    for start, size in row_chunks(hours, 512):
        columns = slice(start, start + size)
        sums = lax.dot_general(stacked, z_ref[:, columns], NN, preferred_element_type=F32)
        out_ref[:, columns] = sums[:modes] + (sums[modes : 2 * modes] + sums[2 * modes :])


def temp_sums(temp, split, weight):
    blocks, cells, width = temp.shape
    modes = split.shape[0] // 3
    scores = pl.pallas_call(
        scores_kernel,
        out_shape=jax.ShapeDtypeStruct((cells, blocks * width), BF16),
        compiler_params=params(),
        cost_estimate=pl.CostEstimate(
            flops=16 * temp.size, bytes_accessed=4 * temp.size, transcendentals=cells
        ),
    )(temp, weight)
    return pl.pallas_call(
        sums_kernel,
        out_shape=jax.ShapeDtypeStruct((modes, blocks * width), F32),
        compiler_params=params(),
        cost_estimate=pl.CostEstimate(
            flops=12 * cells * modes * blocks * width,
            bytes_accessed=2 * temp.size + 2 * split.size,
            transcendentals=0,
        ),
    )(scores, split)


def sum_kernel(got_ref, out_ref):
    count = got_ref.shape[0]
    parts = []
    for n in range(8):
        part = got_ref[n]
        for m in range(n + 8, count, 8):
            part = part + got_ref[m]
        parts.append(part)
    while len(parts) > 1:
        parts = [parts[n] + parts[n + 1] for n in range(0, len(parts), 2)]
    for n in range(out_ref.shape[0]):
        out_ref[n] = parts[0]


def sum_for_all(got, copies):
    return pl.pallas_call(
        sum_kernel,
        out_shape=jax.ShapeDtypeStruct((copies, *got.shape[1:]), F32),
        compiler_params=params(),
        cost_estimate=pl.CostEstimate(flops=got.size, bytes_accessed=8 * got.size, transcendentals=0),
    )(got)


def band_kernel(place_ref, h_ref, out_ref):
    lons, lats, width = h_ref.shape
    low = lax.broadcasted_iota(jnp.int32, (1, 8, width), 1) < 4
    for start, size in row_chunks(lons, 16):
        for top in range(0, lats, 16):
            tiles = h_ref[start : start + size, top : top + 16, :].astype(F32)
            for q in range(2):
                pairs = tiles[:, 8 * q : 8 * q + 8, :].reshape(size // 2, 2, 8, width)
                even, odd = pairs[:, 0], pairs[:, 1]
                first = jnp.where(low, even, jnp.roll(odd, 4, axis=1))
                second = jnp.where(low, jnp.roll(even, 4, axis=1), odd)
                rows = slice(4 * start, 4 * (start + size))
                band = top // 4 + 2 * q
                out_ref[place_ref[band], rows, :] = first.reshape(4 * size, width).astype(BF16)
                out_ref[place_ref[band + 1], rows, :] = second.reshape(4 * size, width).astype(BF16)


def lay_out_bands(places, hum):
    lons, lats, width = hum.shape
    return pl.pallas_call(
        band_kernel,
        in_specs=[pl.BlockSpec(memory_space=pltpu.SMEM), pl.BlockSpec(memory_space=pltpu.VMEM)],
        out_shape=jax.ShapeDtypeStruct((lats // 4, 4 * lons, width), BF16),
        compiler_params=params(),
        cost_estimate=pl.CostEstimate(flops=0, bytes_accessed=4 * hum.size, transcendentals=0),
    )(places, hum)


def hum_kernel(place_ref, *refs):
    pieces, out_ref = refs[:-1], refs[-1]
    count = len(pieces)
    _, cells, width = pieces[0].shape
    hours = count * width
    for start, size in row_chunks(cells, 48):
        rows = slice(start, start + size)
        total = jnp.zeros((size, width), F32)
        for piece in pieces:
            total = total + piece[0, rows, :].astype(F32)
        average = jnp.sum(total, axis=1, keepdims=True) / hours
        square = jnp.zeros((size, width), F32)
        for piece in pieces:
            centered = piece[0, rows, :].astype(F32) - average
            square = square + centered * centered
        scale = lax.rsqrt(jnp.sum(square, axis=1, keepdims=True) / hours + EPS)
        for n, piece in enumerate(pieces):
            centered = piece[0, rows, :].astype(F32) - average
            columns = pl.ds(pl.multiple_of(place_ref[n] * width, width), width)
            out_ref[rows, columns] = (centered * scale).astype(BF16)


def hum_scores(places, pieces):
    count = len(pieces)
    _, cells, width = pieces[0].shape
    return pl.pallas_call(
        hum_kernel,
        in_specs=[pl.BlockSpec(memory_space=pltpu.SMEM)]
        + [pl.BlockSpec(memory_space=pltpu.VMEM)] * count,
        out_shape=jax.ShapeDtypeStruct((cells, count * width), BF16),
        compiler_params=params(),
        cost_estimate=pl.CostEstimate(
            flops=0, bytes_accessed=16 * cells * width * count, transcendentals=0
        ),
    )(places, *pieces)


def correlations(pcs_ref, z_ref, factor_ref, rows_ref):
    octets, runs, _, _ = pcs_ref.shape
    lats, lons = factor_ref.shape
    modes, hours = 8 * octets, runs * 128
    rows = []
    for r in range(octets):
        pcs = jnp.concatenate([pcs_ref[r, c] for c in range(runs)], axis=1)
        centered = pcs - jnp.sum(pcs, axis=1, keepdims=True) / hours
        variance = jnp.sum(centered * centered, axis=1, keepdims=True) / hours
        rows.append(centered * lax.rsqrt(variance + EPS))
    pcz = jnp.concatenate(rows, axis=0).astype(BF16)
    rows_ref[:, :modes] = lax.dot_general(z_ref[...], pcz, NT, preferred_element_type=F32)
    return [
        rows_ref[pl.ds(i, lons, stride=lats), :].T[:modes] * factor_ref[i : i + 1, :]
        for i in range(lats)
    ]


def own_kernel(pcs_ref, z_ref, factor_ref, out_ref, rows_ref):
    for i, values in enumerate(correlations(pcs_ref, z_ref, factor_ref, rows_ref)):
        out_ref[i] = values


def both_kernel(core_ref, pcs_ref, z_ref, factor_ref, own_ref, out_ref, rows_ref):
    core = core_ref[0]
    for i, other in enumerate(correlations(pcs_ref, z_ref, factor_ref, rows_ref)):
        own = own_ref[i]
        for r in range(out_ref.shape[1] // 8):
            half = slice(8 * (r // 2), 8 * (r // 2) + 8)
            out_ref[i, 8 * r : 8 * r + 8, :] = jnp.where(core == r % 2, own[half], other[half])


def correlate(core, own, other, scores, factor):
    lats, lons = factor.shape
    modes = own.shape[0] * own.shape[2]
    vmem = pl.BlockSpec(memory_space=pltpu.VMEM)
    settings = dict(
        scratch_shapes=[pltpu.VMEM((lats * lons, 128), F32)],
        compiler_params=params(),
        cost_estimate=pl.CostEstimate(
            flops=2 * scores.size * modes, bytes_accessed=4 * own.size + 2 * scores.size, transcendentals=0
        ),
    )
    first = pl.pallas_call(
        own_kernel, out_shape=jax.ShapeDtypeStruct((lats, modes, lons), F32), **settings
    )(own, scores, factor)
    return pl.pallas_call(
        both_kernel,
        in_specs=[pl.BlockSpec(memory_space=pltpu.SMEM), vmem, vmem, vmem, vmem],
        out_shape=jax.ShapeDtypeStruct((lats, 2 * modes, lons), F32),
        **settings,
    )(core.reshape(1), other, scores, factor, first)


def area_root(rows, total_lat):
    latitude = ((rows.astype(F32) + 0.5) / total_lat * 120.0 - 60.0) * (math.pi / 180.0)
    return jnp.sqrt(jnp.cos(latitude))


def per_device(thermal_reading, moisture_content, gram_eigenvector_columns, marine_indicator):
    total_lat, lons, width = thermal_reading.shape
    lats = marine_indicator.shape[0]
    hours, modes = gram_eigenvector_columns.shape
    members = lax.axis_size("tm")
    others = lax.axis_size("space")
    chips = members // 2
    me = lax.axis_index("tm")
    chip, core = lax.div(me, 2), lax.rem(me, 2)
    to_core = [(n, n ^ 1) for n in range(members)]
    to_chip = [[(n, (n + 2 * d) % members) for n in range(members)] for d in range(chips)]
    mask_float = marine_indicator.astype(F32)

    half = lons // 2
    temp = thermal_reading.transpose(1, 0, 2).reshape(2, half, chips, 8, width)
    temp = pack_octets(temp).reshape(members, 8 * half, width)
    temp = lax.all_to_all(temp, "tm", 0, 0)

    band = jnp.arange(members, dtype=jnp.int32)
    far = lax.rem(lax.div(band, 2) + 2 * chips - chip - 1, chips)
    order = 2 * far + lax.rem(band + core, 2)
    laid = lay_out_bands(order, moisture_content.transpose(1, 0, 2))
    sent, own = [laid[2 * d : 2 * d + 2] for d in range(chips - 1)], laid[2 * chips - 2 :]

    other = lax.ppermute(marine_indicator, "tm", to_core)
    pair = jnp.where(core == 0, jnp.stack([marine_indicator, other]), jnp.stack([other, marine_indicator]))
    pair, *sent = lax.optimization_barrier((pair, *sent))
    arrived = [lax.ppermute(sent[d - 1], "tm", to_chip[d]) for d in range(1, chips)]
    root = area_root(8 * chip + jnp.arange(8, dtype=jnp.int32), total_lat)
    scaling = root[:, None] * pair.reshape(8, lons).astype(F32)
    weight = lax.dynamic_slice(scaling.T, (core * half, 0), (half, 8)).reshape(1, 8 * half)

    partial_t = temp_sums(temp, split_columns(gram_eigenvector_columns.T), weight)
    blocks = partial_t.reshape(modes // 8, 8, hours // 128, 128)
    blocks = blocks.transpose(0, 2, 1, 3).reshape(-1, 8, 128)
    got = lax.all_to_all(blocks, BOTH, 0, 0)
    traded = [lax.ppermute(blocks[1:2], "tm", to_core) for blocks in [own, *arrived]]
    pieces = [piece for both in zip([own, *arrived], traded) for piece in both]
    places = 2 * lax.rem(chip + chips - lax.div(band, 2), chips) + lax.rem(band + core, 2)
    scores = hum_scores(places, pieces)
    got, scores = lax.optimization_barrier((got, scores))
    kinds = [
        [t * others + n for t in range(kind, members, 2) for n in range(others)] for kind in range(2)
    ]
    pcs = lax.all_to_all(sum_for_all(got, chips * others), BOTH, 0, 0, axis_index_groups=kinds)
    pcs = pcs.reshape(chips, others, 8, 128)
    pcs_other = lax.ppermute(pcs, "tm", to_core)

    return correlate(core, pcs, pcs_other, scores, mask_float / hours).transpose(0, 2, 1)


def solution(mesh):
    in_specs = (P(None, "space", "tm"), P(None, "space", "tm"), P(), P("tm", "space"))
    out_specs = P("tm", "space", None)
    return jax.shard_map(
        per_device, mesh=mesh, in_specs=in_specs, out_specs=out_specs, check_vma=False
    )
```

```python
import math

import jax
import jax.numpy as jnp
from jax import lax
from jax.experimental import pallas as pl
from jax.experimental.pallas import tpu as pltpu
from jax.sharding import PartitionSpec as P

BOTH = ("tm", "space")
F32 = jnp.float32
BF16 = jnp.bfloat16
EPS = 1e-05
PACK_VMEM = 56 * 1024 * 1024
PARTS = 3
NT = (((1,), (1,)), ((), ()))
NN = (((1,), (0,)), ((), ()))


def params():
    return pltpu.CompilerParams(vmem_limit_bytes=16 * 1024 * 1024)


def row_chunks(rows, step):
    return [(start, min(step, rows - start)) for start in range(0, rows, step)]


def three_terms(x):
    high = x.astype(BF16)
    rest = x - high.astype(F32)
    middle = rest.astype(BF16)
    low = (rest - middle.astype(F32)).astype(BF16)
    return high, middle, low


def pack_kernel(in_ref, out_ref, held, loaded, stored):
    halves, lons, octets, _, _ = in_ref.shape
    part = lons // PARTS
    places = [
        (o, h, slice(p * part, (p + 1) * part if p < PARTS - 1 else lons))
        for o in range(octets)
        for h in range(halves)
        for p in range(PARTS)
    ]
    loads = [
        pltpu.make_async_copy(in_ref.at[h, run, o], held.at[o, h, run], loaded.at[n])
        for n, (o, h, run) in enumerate(places)
    ]
    stores = [
        pltpu.make_async_copy(held.at[o, h, run], out_ref.at[o, h, run], stored.at[n])
        for n, (o, h, run) in enumerate(places)
    ]
    for load in loads:
        load.start()
    for load, store in zip(loads, stores):
        load.wait()
        store.start()
    for store in stores:
        store.wait()


def pack_octets(field):
    halves, lons, octets, rows, width = field.shape
    shape = (octets, halves, lons, rows, width)
    return pl.pallas_call(
        pack_kernel,
        in_specs=[pl.BlockSpec(memory_space=pl.ANY)],
        out_specs=pl.BlockSpec(memory_space=pl.ANY),
        out_shape=jax.ShapeDtypeStruct(shape, field.dtype),
        scratch_shapes=[
            pltpu.VMEM(shape, field.dtype),
            pltpu.SemaphoreType.DMA((octets * halves * PARTS,)),
            pltpu.SemaphoreType.DMA((octets * halves * PARTS,)),
        ],
        compiler_params=pltpu.CompilerParams(vmem_limit_bytes=PACK_VMEM),
        cost_estimate=pl.CostEstimate(flops=0, bytes_accessed=4 * field.size, transcendentals=0),
    )(field)


def split_kernel(modes, e_ref, out_ref):
    for n, term in enumerate(three_terms(e_ref[...])):
        out_ref[n * modes : (n + 1) * modes, :] = term


def split_columns(columns_t):
    modes, hours = columns_t.shape
    return pl.pallas_call(
        lambda e_ref, out_ref: split_kernel(modes, e_ref, out_ref),
        out_shape=jax.ShapeDtypeStruct((3 * modes, hours), BF16),
        compiler_params=params(),
        cost_estimate=pl.CostEstimate(flops=0, bytes_accessed=5 * modes * hours * 2, transcendentals=0),
    )(columns_t)


def scores_kernel(t_ref, w_ref, z_ref):
    blocks, cells, width = t_ref.shape
    hours = blocks * width
    weights = jnp.broadcast_to(w_ref[...], (128, cells)).T
    for start, size in row_chunks(cells, 48):
        rows = slice(start, start + size)
        total = jnp.zeros((size, width), F32)
        for b in range(blocks):
            total = total + t_ref[b, rows, :].astype(F32)
        average = jnp.sum(total, axis=1, keepdims=True) / hours
        square = jnp.zeros((size, width), F32)
        for b in range(blocks):
            centered = t_ref[b, rows, :].astype(F32) - average
            square = square + centered * centered
        scale = lax.rsqrt(jnp.sum(square, axis=1, keepdims=True) / hours + EPS)
        weight = weights[rows, :1]
        for b in range(blocks):
            centered = t_ref[b, rows, :].astype(F32) - average
            z_ref[rows, b * width : (b + 1) * width] = ((centered * scale) * weight).astype(BF16)


def column_sums(stacked, z_ref, out_ref):
    modes, hours = out_ref.shape
    for start, size in row_chunks(hours, 512):
        columns = slice(start, start + size)
        sums = lax.dot_general(stacked, z_ref[:, columns], NN, preferred_element_type=F32)
        out_ref[:, columns] = sums[:modes] + (sums[modes : 2 * modes] + sums[2 * modes :])


def other_kernel(core_ref, z_ref, e_ref, out_ref, own_ref):
    modes = 2 * out_ref.shape[0]
    turned = lax.dot_general(e_ref[...], z_ref[...], NT, preferred_element_type=F32)
    turned = turned[:modes] + (turned[modes : 2 * modes] + turned[2 * modes :])
    even = jnp.concatenate([turned[n : n + 8] for n in range(0, modes, 16)], axis=0)
    odd = jnp.concatenate([turned[n : n + 8] for n in range(8, modes, 16)], axis=0)
    first = core_ref[0] == 0
    own_ref[...] = jnp.concatenate(three_terms(jnp.where(first, even, odd)), axis=0)
    column_sums(jnp.concatenate(three_terms(jnp.where(first, odd, even)), axis=0), z_ref, out_ref)


def own_sums_kernel(stacked_ref, z_ref, out_ref):
    column_sums(stacked_ref[...], z_ref, out_ref)


def temp_sums(core, temp, split, weight):
    blocks, cells, width = temp.shape
    modes, hours = split.shape[0] // 6, blocks * width
    scores = pl.pallas_call(
        scores_kernel,
        out_shape=jax.ShapeDtypeStruct((cells, hours), BF16),
        compiler_params=params(),
        cost_estimate=pl.CostEstimate(
            flops=16 * temp.size, bytes_accessed=4 * temp.size, transcendentals=cells
        ),
    )(temp, weight)
    cost = pl.CostEstimate(
        flops=6 * cells * modes * hours, bytes_accessed=2 * temp.size, transcendentals=0
    )
    vmem = pl.BlockSpec(memory_space=pltpu.VMEM)
    other, stacked = pl.pallas_call(
        other_kernel,
        in_specs=[pl.BlockSpec(memory_space=pltpu.SMEM), vmem, vmem],
        out_shape=(
            jax.ShapeDtypeStruct((modes, hours), F32),
            jax.ShapeDtypeStruct((3 * modes, cells), BF16),
        ),
        compiler_params=params(),
        cost_estimate=cost,
    )(core.reshape(1), scores, split)
    own = pl.pallas_call(
        own_sums_kernel,
        out_shape=jax.ShapeDtypeStruct((modes, hours), F32),
        compiler_params=params(),
        cost_estimate=cost,
    )(stacked, scores)
    return own, other


def sum_kernel(got_ref, out_ref):
    count = got_ref.shape[0]
    parts = []
    for n in range(8):
        part = got_ref[n]
        for m in range(n + 8, count, 8):
            part = part + got_ref[m]
        parts.append(part)
    while len(parts) > 1:
        parts = [parts[n] + parts[n + 1] for n in range(0, len(parts), 2)]
    for n in range(out_ref.shape[0]):
        out_ref[n] = parts[0]


def sum_for_all(got, copies):
    return pl.pallas_call(
        sum_kernel,
        out_shape=jax.ShapeDtypeStruct((copies, *got.shape[1:]), F32),
        compiler_params=params(),
        cost_estimate=pl.CostEstimate(flops=got.size, bytes_accessed=8 * got.size, transcendentals=0),
    )(got)


def band_kernel(place_ref, h_ref, out_ref):
    lons, lats, width = h_ref.shape
    low = lax.broadcasted_iota(jnp.int32, (1, 8, width), 1) < 4
    for start, size in row_chunks(lons, 16):
        for top in range(0, lats, 16):
            tiles = h_ref[start : start + size, top : top + 16, :].astype(F32)
            for q in range(2):
                pairs = tiles[:, 8 * q : 8 * q + 8, :].reshape(size // 2, 2, 8, width)
                even, odd = pairs[:, 0], pairs[:, 1]
                first = jnp.where(low, even, jnp.roll(odd, 4, axis=1))
                second = jnp.where(low, jnp.roll(even, 4, axis=1), odd)
                rows = slice(4 * start, 4 * (start + size))
                band = top // 4 + 2 * q
                out_ref[place_ref[band], rows, :] = first.reshape(4 * size, width).astype(BF16)
                out_ref[place_ref[band + 1], rows, :] = second.reshape(4 * size, width).astype(BF16)


def lay_out_bands(places, hum):
    lons, lats, width = hum.shape
    return pl.pallas_call(
        band_kernel,
        in_specs=[pl.BlockSpec(memory_space=pltpu.SMEM), pl.BlockSpec(memory_space=pltpu.VMEM)],
        out_shape=jax.ShapeDtypeStruct((lats // 4, 4 * lons, width), BF16),
        compiler_params=params(),
        cost_estimate=pl.CostEstimate(flops=0, bytes_accessed=4 * hum.size, transcendentals=0),
    )(places, hum)


def hum_kernel(place_ref, *refs):
    pieces, out_ref = refs[:-1], refs[-1]
    count = len(pieces)
    _, cells, width = pieces[0].shape
    hours = count * width
    for start, size in row_chunks(cells, 48):
        rows = slice(start, start + size)
        total = jnp.zeros((size, width), F32)
        for piece in pieces:
            total = total + piece[0, rows, :].astype(F32)
        average = jnp.sum(total, axis=1, keepdims=True) / hours
        square = jnp.zeros((size, width), F32)
        for piece in pieces:
            centered = piece[0, rows, :].astype(F32) - average
            square = square + centered * centered
        scale = lax.rsqrt(jnp.sum(square, axis=1, keepdims=True) / hours + EPS)
        for n, piece in enumerate(pieces):
            centered = piece[0, rows, :].astype(F32) - average
            columns = pl.ds(pl.multiple_of(place_ref[n] * width, width), width)
            out_ref[rows, columns] = (centered * scale).astype(BF16)


def hum_scores(places, pieces):
    count = len(pieces)
    _, cells, width = pieces[0].shape
    return pl.pallas_call(
        hum_kernel,
        in_specs=[pl.BlockSpec(memory_space=pltpu.SMEM)]
        + [pl.BlockSpec(memory_space=pltpu.VMEM)] * count,
        out_shape=jax.ShapeDtypeStruct((cells, count * width), BF16),
        compiler_params=params(),
        cost_estimate=pl.CostEstimate(
            flops=0, bytes_accessed=16 * cells * width * count, transcendentals=0
        ),
    )(places, *pieces)


def correlations(pcs_ref, z_ref, factor_ref, rows_ref):
    octets, runs, _, _ = pcs_ref.shape
    lats, lons = factor_ref.shape
    modes, hours = 8 * octets, runs * 128
    rows = []
    for r in range(octets):
        pcs = jnp.concatenate([pcs_ref[r, c] for c in range(runs)], axis=1)
        centered = pcs - jnp.sum(pcs, axis=1, keepdims=True) / hours
        variance = jnp.sum(centered * centered, axis=1, keepdims=True) / hours
        rows.append(centered * lax.rsqrt(variance + EPS))
    pcz = jnp.concatenate(rows, axis=0).astype(BF16)
    rows_ref[:, :modes] = lax.dot_general(z_ref[...], pcz, NT, preferred_element_type=F32)
    return [
        rows_ref[pl.ds(i, lons, stride=lats), :].T[:modes] * factor_ref[i : i + 1, :]
        for i in range(lats)
    ]


def own_kernel(pcs_ref, z_ref, factor_ref, out_ref, rows_ref):
    for i, values in enumerate(correlations(pcs_ref, z_ref, factor_ref, rows_ref)):
        out_ref[i] = values


def both_kernel(core_ref, pcs_ref, z_ref, factor_ref, own_ref, out_ref, rows_ref):
    core = core_ref[0]
    for i, other in enumerate(correlations(pcs_ref, z_ref, factor_ref, rows_ref)):
        own = own_ref[i]
        for r in range(out_ref.shape[1] // 8):
            half = slice(8 * (r // 2), 8 * (r // 2) + 8)
            out_ref[i, 8 * r : 8 * r + 8, :] = jnp.where(core == r % 2, own[half], other[half])


def correlate(core, own, other, scores, factor):
    lats, lons = factor.shape
    modes = own.shape[0] * own.shape[2]
    vmem = pl.BlockSpec(memory_space=pltpu.VMEM)
    settings = dict(
        scratch_shapes=[pltpu.VMEM((lats * lons, 128), F32)],
        compiler_params=params(),
        cost_estimate=pl.CostEstimate(
            flops=2 * scores.size * modes, bytes_accessed=4 * own.size + 2 * scores.size, transcendentals=0
        ),
    )
    first = pl.pallas_call(
        own_kernel, out_shape=jax.ShapeDtypeStruct((lats, modes, lons), F32), **settings
    )(own, scores, factor)
    return pl.pallas_call(
        both_kernel,
        in_specs=[pl.BlockSpec(memory_space=pltpu.SMEM), vmem, vmem, vmem, vmem],
        out_shape=jax.ShapeDtypeStruct((lats, 2 * modes, lons), F32),
        **settings,
    )(core.reshape(1), other, scores, factor, first)


def area_root(rows, total_lat):
    latitude = ((rows.astype(F32) + 0.5) / total_lat * 120.0 - 60.0) * (math.pi / 180.0)
    return jnp.sqrt(jnp.cos(latitude))


def per_device(thermal_reading, moisture_content, gram_eigenvector_columns, marine_indicator):
    total_lat, lons, width = thermal_reading.shape
    lats = marine_indicator.shape[0]
    hours, modes = gram_eigenvector_columns.shape
    members = lax.axis_size("tm")
    others = lax.axis_size("space")
    chips = members // 2
    me = lax.axis_index("tm")
    chip, core = lax.div(me, 2), lax.rem(me, 2)
    to_core = [(n, n ^ 1) for n in range(members)]
    to_chip = [[(n, (n + 2 * d) % members) for n in range(members)] for d in range(chips)]
    mask_float = marine_indicator.astype(F32)

    half = lons // 2
    temp = thermal_reading.transpose(1, 0, 2).reshape(2, half, chips, 8, width)
    temp = pack_octets(temp).reshape(members, 8 * half, width)
    temp = lax.all_to_all(temp, "tm", 0, 0)

    band = jnp.arange(members, dtype=jnp.int32)
    far = lax.rem(lax.div(band, 2) + 2 * chips - chip - 1, chips)
    order = 2 * far + lax.rem(band + core, 2)
    laid = lay_out_bands(order, moisture_content.transpose(1, 0, 2))
    sent, own = [laid[2 * d : 2 * d + 2] for d in range(chips - 1)], laid[2 * chips - 2 :]

    other = lax.ppermute(marine_indicator, "tm", to_core)
    pair = jnp.where(core == 0, jnp.stack([marine_indicator, other]), jnp.stack([other, marine_indicator]))
    pair, *sent = lax.optimization_barrier((pair, *sent))
    arrived = [lax.ppermute(sent[d - 1], "tm", to_chip[d]) for d in range(1, chips)]
    root = area_root(8 * chip + jnp.arange(8, dtype=jnp.int32), total_lat)
    scaling = root[:, None] * pair.reshape(8, lons).astype(F32)
    weight = lax.dynamic_slice(scaling.T, (core * half, 0), (half, 8)).reshape(1, 8 * half)

    own_sums, other_sums = temp_sums(core, temp, split_columns(gram_eigenvector_columns.T), weight)
    partial_t = own_sums + lax.ppermute(other_sums, "tm", to_core)
    blocks = partial_t.reshape(chips, 8, others, 128).transpose(0, 2, 1, 3).reshape(-1, 8, 128)
    kinds = [
        [t * others + n for t in range(kind, members, 2) for n in range(others)] for kind in range(2)
    ]
    got = lax.all_to_all(blocks, BOTH, 0, 0, axis_index_groups=kinds)
    traded = [lax.ppermute(blocks[1:2], "tm", to_core) for blocks in [own, *arrived]]
    pieces = [piece for both in zip([own, *arrived], traded) for piece in both]
    places = 2 * lax.rem(chip + chips - lax.div(band, 2), chips) + lax.rem(band + core, 2)
    scores = hum_scores(places, pieces)
    got, scores = lax.optimization_barrier((got, scores))
    pcs = lax.all_to_all(sum_for_all(got, chips * others), BOTH, 0, 0, axis_index_groups=kinds)
    pcs = pcs.reshape(chips, others, 8, 128)
    pcs_other = lax.ppermute(pcs, "tm", to_core)

    return correlate(core, pcs, pcs_other, scores, mask_float / hours).transpose(0, 2, 1)


def solution(mesh):
    in_specs = (P(None, "space", "tm"), P(None, "space", "tm"), P(), P("tm", "space"))
    out_specs = P("tm", "space", None)
    return jax.shard_map(
        per_device, mesh=mesh, in_specs=in_specs, out_specs=out_specs, check_vma=False
    )
```
